32 devices in a mesh: ctx: 8 (over z, core), tp: 4 (over y, x).
Axes of the slice: x: 2, y: 2, z: 4, core: 2. Of those that a mesh axis runs over, the one named last changes fastest.
Arguments:
- queries: bfloat16 [2048, 8192], P('ctx', 'tp'), may hold values from -6 to 6
- keys: bfloat16 [2048, 8192], P('ctx', 'tp'), may hold values from -0.125 to 0.125
- values: bfloat16 [2048, 8192], P('ctx', 'tp'), may hold values from -6 to 6
- log_keep: float32 [64, 2048], P('tp', 'ctx'), may hold values from -1 to 0, as said below
- state_in: float32 [64, 128, 128], P('tp'), may hold values from -6 to 6
- norm_gain: float32 [8192], P('tp'), may hold values from 0.1 to 1.9
- out_weight: bfloat16 [8192, 6144], P('tp', 'ctx'), may hold values from -0.09375 to 0.09375
Outputs:
- normed: bfloat16 [2048, 8192], P('ctx', 'tp')
- state_out: float32 [64, 128, 128], P('tp', 'ctx')
- layer_out: bfloat16 [2048, 6144], P('ctx', 'tp')
The draws below stay inside these ranges and needn't reach their ends.
Inputs may be any that keep to these rules, and one draw needn't show every extreme that they name: `log_keep`: every entry is a logarithm of a keep factor, so at most 0.
All inputs are finite; a program needn't handle non-finite values.
Results may differ from the reference program's by a relative error of at most 0.014.
Values may be sent and summed in bfloat16 or wider, within the bound.
A program may use at most 128 MiB of HBM per device.

```python
import jax
import jax.numpy as jnp
from jax import lax

H = 64
DH = 128
D = 6144
SPAN = 256
TOKENS = 2048
N_TP = 4


def draw_log_keep(key, part):
    k_fast, k_quick, k_slow, k_spots, k_depth = jax.random.split(key, 5)
    share = 0.5
    fast = jax.random.bernoulli(k_fast, share, (H,))
    quick_rate = jnp.exp(jax.random.uniform(k_quick, (H,), jnp.float32, jnp.log(1.0 / 50.0), jnp.log(1.0 / 30.0)))
    slow_rate = jnp.exp(jax.random.uniform(k_slow, (H,), jnp.float32, jnp.log(0.05), jnp.log(0.5))) / TOKENS
    decay_rate = jnp.where(fast, quick_rate, slow_rate)
    token_positions = jax.random.randint(k_spots, (2, H), 0, TOKENS)
    layer_depth = jax.random.uniform(k_depth, (2, H), jnp.float32, jnp.log(0.5), jnp.log(0.8))
    part_positions = jnp.arange(TOKENS)
    block_length = jnp.where(part_positions[None, :] == token_positions[0][:, None], layer_depth[0][:, None], 0.0)
    block_length = block_length + jnp.where(part_positions[None, :] == token_positions[1][:, None], layer_depth[1][:, None], 0.0)
    return jnp.maximum(block_length - decay_rate[:, None], -1.0).astype(jnp.float32)


def spiked(array, rng, source, target, parts, factor):
    def block_of(position):
        return (jnp.arange(array.shape[position]) // (array.shape[position] // parts)).reshape((-1,) + (1,) * (array.ndim - 1 - position))

    near = jax.random.permutation(rng, parts)[block_of(target)]
    far = (block_of(target) + parts // 2) % parts
    return jnp.where((block_of(source) == near) | (block_of(source) == far), factor * array, array)


def block_scale(rng, dims, cuts, least, largest):
    factor_of = 1.0
    for position, parts in cuts:
        draws = jax.random.uniform(jax.random.fold_in(jax.random.fold_in(rng, 6), position), (parts,), jnp.float32, least / len(cuts), largest / len(cuts))
        factor_of = factor_of * jnp.repeat(jnp.exp(draws), dims[position] // parts).reshape((-1,) + (1,) * (len(dims) - 1 - position))
    return factor_of


def gaussian(own_key, dims, scale, limit, cuts=(), kind=jnp.bfloat16):
    array = scale * jax.random.normal(own_key, dims, jnp.float32)
    if cuts:
        array = array * block_scale(own_key, dims, cuts, -0.22, 0.18)
    return jnp.clip(array, -limit, limit).astype(kind)


def noise_with(own_key, dims, scale, reach, pieces, heavy, kind=jnp.bfloat16):
    result = scale * jax.random.normal(own_key, dims, jnp.float32)
    if pieces:
        result = result * block_scale(own_key, dims, pieces, -0.22, 0.18)
    return jnp.clip(spiked(result, jax.random.fold_in(own_key, 3), *heavy), -reach, reach).astype(kind)


def setup_inputs(seed: int = 0) -> dict:
    key_of = jax.random.split(jax.random.key(seed), 8)
    return {
        "queries": gaussian(key_of[0], (TOKENS, H * DH), 1.0, 6.0, ((0, 8), (1, 4))),
        "keys": gaussian(key_of[1], (TOKENS, H * DH), TOKENS ** -0.5, 0.125, ((0, 8), (1, 4))),
        "values": gaussian(key_of[2], (TOKENS, H * DH), 1.0, 6.0, ((0, 8), (1, 4))),
        "log_keep": draw_log_keep(jax.random.fold_in(key_of[7], 71), 0),
        "state_in": gaussian(key_of[4], (H, DH, DH), 1.0, 6.0, ((0, 4),), jnp.float32),
        "norm_gain": jnp.clip(1.0 + 0.18 * jax.random.normal(key_of[5], (H * DH,), jnp.float32), 0.1, 1.9),
        "out_weight": noise_with(key_of[6], (H * DH, D), (H * DH) ** -0.5, 0.09375, ((0, 4), (1, 8)), (0, 1, 8, 2.0)),
    }


def reference(queries, keys, values, log_keep, state_in, norm_gain, out_weight):
    blocks = TOKENS // SPAN
    q_all = queries.reshape(blocks, SPAN, H, DH)
    k_all = keys.reshape(blocks, SPAN, H, DH)
    v_all = values.reshape(blocks, SPAN, H, DH)
    logs = log_keep.reshape(H, blocks, SPAN).transpose(1, 0, 2)
    causal = jnp.tril(jnp.ones((SPAN, SPAN), dtype=bool))

    def advance(state, item):
        q_blk, k_blk, v_blk, log_blk = item
        q_f = q_blk.astype(jnp.float32)
        k_f = k_blk.astype(jnp.float32)
        v_f = v_blk.astype(jnp.float32)
        within = jnp.cumsum(log_blk, axis=1)
        spread = within[:, :, None] - within[:, None, :]
        decay = jnp.where(causal[None], jnp.exp(jnp.minimum(spread, 0.0)), 0.0)
        scores = jnp.einsum('shd,thd->hst', q_f, k_f)
        weights = lax.optimization_barrier((scores * decay).astype(jnp.bfloat16))
        intra = jnp.einsum('hst,thd->shd', weights.astype(jnp.float32), v_f)
        start = lax.optimization_barrier(state.astype(jnp.bfloat16))
        inter = jnp.einsum('shd,hde->she', q_f, start.astype(jnp.float32)) * jnp.exp(within).T[:, :, None]
        total = within[:, -1]
        keys_decayed = lax.optimization_barrier((k_f * jnp.exp(total[:, None] - within).T[:, :, None]).astype(jnp.bfloat16))
        increment = jnp.einsum('shd,she->hde', keys_decayed.astype(jnp.float32), v_f)
        state = jnp.exp(total)[:, None, None] * state + increment
        return (state, intra + inter)
    state_out, outs = lax.scan(advance, state_in, (q_all, k_all, v_all, logs))
    attended = outs.reshape(TOKENS, H * DH)
    mean_square = lax.optimization_barrier(jnp.mean(attended * attended, axis=1))
    normed = (attended * lax.rsqrt(mean_square + 1e-06)[:, None] * norm_gain).astype(jnp.bfloat16)
    group = H * DH // N_TP
    normed_parts = normed.reshape(TOKENS, N_TP, group).transpose(1, 0, 2)
    weight_parts = out_weight.reshape(N_TP, group, D)

    def add_group(total_sum, item):
        left, right = item
        partial_value = jnp.dot(left, right, preferred_element_type=jnp.float32)
        rounded = lax.optimization_barrier(partial_value.astype(jnp.bfloat16))
        return (total_sum + rounded.astype(jnp.float32), None)
    summed, unused = lax.scan(add_group, jnp.zeros((TOKENS, D), jnp.float32), (normed_parts, weight_parts))
    return (normed, state_out, summed.astype(jnp.bfloat16))
```

```python
import functools

import jax
import jax.numpy as jnp
from jax import lax
from jax.experimental import pallas as pl
from jax.experimental.pallas import tpu as pltpu
from jax.sharding import PartitionSpec as P

EPSILON = 1e-06
HIGH = lax.Precision.HIGHEST
MESH = pl.DeviceIdType.MESH
F32 = jnp.float32
BF16 = jnp.bfloat16


def wait_bytes(ref, sem):
    pltpu.make_async_copy(ref, ref, sem).wait()


def dot(a, b, over, precision=None):
    return lax.dot_general(
        a, b, (over, ((), ())), precision=precision, preferred_element_type=F32
    )


def kernel(
    peers, groups, chunks,
    q, k, v, logs, s_in, gain, w_hbm,
    normed, state, layer,
    w, padded, brow, bcol, inc, zst, att, cin, cout, shares, ssq_out, ssq_in,
    acts, parts, arrived, summed,
    w_sem, chain_s, chain_r, st_s, st_r, sq_s, sq_r, a_s, a_r, rs_s, rs_r, fin_s, fin_r,
):
    c = lax.axis_index("ctx")
    t = lax.axis_index("tp")
    heads, tokens = logs.shape
    width = s_in.shape[1]
    share = state.shape[0] // heads
    chips = peers // 2
    z, j = c // 2, c % 2
    ratio = peers // groups
    rows_here = tokens // groups
    per_chunk = heads // chunks
    last = peers - 1

    def remote(src, dst, send, recv, ctx, tp):
        return pltpu.make_async_remote_copy(
            src_ref=src, dst_ref=dst, send_sem=send, recv_sem=recv,
            device_id={"ctx": ctx, "tp": tp}, device_id_type=MESH,
        )

    w_copy = pltpu.make_async_copy(w_hbm, w, w_sem)
    w_copy.start()
    barrier = pltpu.get_barrier_semaphore()
    everyone = peers * groups

    def greet(i, carry):
        other = (c * groups + t + i) % everyone
        pl.semaphore_signal(
            barrier, inc=1,
            device_id={"ctx": other // groups, "tp": other % groups},
            device_id_type=MESH,
        )
        return carry

    lax.fori_loop(1, everyone, greet, 0)

    padded[...] = jnp.zeros_like(padded)
    padded[0:heads, :] = logs[...]
    rows = lax.broadcasted_iota(jnp.int32, (tokens, tokens), 0)
    cols = lax.broadcasted_iota(jnp.int32, (tokens, tokens), 1)
    upper = jnp.where(rows <= cols, 1.0, 0.0).astype(F32)
    by_row = dot(padded[...], upper, ((1,), (0,)), HIGH)
    brow[...] = by_row
    bcol[...] = by_row.T
    lane = lax.broadcasted_iota(jnp.int32, (tokens, 128), 1)

    def column(h):
        return jnp.sum(jnp.where(lane == h, bcol[...], 0.0), axis=1, keepdims=True)

    def head_cols(h):
        return pl.ds(pl.multiple_of(h * width, width), width)

    def head_increment(h, carry):
        hs = head_cols(h)
        summed_logs = column(h)
        factor = jnp.exp(summed_logs[tokens - 1 : tokens] - summed_logs)
        decayed = (k[:, hs].astype(F32) * factor).astype(BF16)
        inc[h] = dot(decayed, v[:, hs], ((0,), (0,)))
        return carry

    lax.fori_loop(0, heads, head_increment, 0, unroll=min(4, heads))
    pl.semaphore_wait(barrier, everyone - 1)

    def chain_copy(g):
        part = pl.ds(g * per_chunk, per_chunk)
        return remote(cout.at[part], cin.at[part], chain_s.at[g], chain_r.at[g], c + 1, t)

    def pass_on(g, incoming):
        for h in range(g * per_chunk, (g + 1) * per_chunk):
            start = incoming[h].astype(F32)
            zst[h] = start
            end = jnp.exp(brow[h : h + 1, tokens - 1 : tokens]) * start + inc[h]
            cout[h] = end.astype(BF16)

            @pl.when(c == last)
            def _():
                for to in range(peers):
                    shares[to, h * share : (h + 1) * share, :] = end[to * share : (to + 1) * share]

        @pl.when(c < last)
        def _():
            chain_copy(g).start()

    @pl.when(c == 0)
    def _():
        for g in range(chunks):
            pass_on(g, s_in)

    causal = rows >= cols

    def head_intra(h, carry):
        hs = head_cols(h)
        scores = dot(q[:, hs], k[:, hs], ((1,), (1,)))
        spread = jnp.minimum(column(h) - brow[pl.ds(h, 1), :], 0.0)
        weights = (scores * jnp.where(causal, jnp.exp(spread), 0.0)).astype(BF16)
        att[:, hs] = dot(weights, v[:, hs], ((1,), (0,)))
        return carry

    lax.fori_loop(0, heads, head_intra, 0, unroll=min(2, heads))

    @pl.when(c > 0)
    def _():
        for g in range(chunks):
            wait_bytes(cin.at[pl.ds(g * per_chunk, per_chunk)], chain_r.at[g])
            pass_on(g, cin)

    def head_inter(h, squares):
        hs = head_cols(h)
        inter = dot(q[:, hs], zst[h].astype(BF16), ((1,), (0,))) * jnp.exp(column(h))
        whole = att[:, hs] + inter
        att[:, hs] = whole
        return squares + whole * whole

    squares = lax.fori_loop(
        0, heads, head_inter, jnp.zeros((tokens, width), F32), unroll=min(4, heads)
    )
    ssq_out[...] = dot(jnp.ones((8, width), F32), squares, ((1,), (1,)), HIGH)
    for off in range(1, groups):
        remote(ssq_out, ssq_in.at[off - 1], sq_s, sq_r, c, (t + off) % groups).start()
    wait_bytes(ssq_in, sq_r)
    total = ssq_out[...]
    for off in range(1, groups):
        total = total + ssq_in[off - 1]
    spread_total = dot(total, jnp.full((8, width), 0.125, F32), ((0,), (0,)), HIGH)
    scale = lax.rsqrt(spread_total / (groups * heads * width) + EPSILON)

    def head_norm(h, carry):
        hs = head_cols(h)
        out = (att[:, hs] * scale * gain[:, hs]).astype(BF16)
        normed[:, hs] = out
        acts[c, :, hs] = out
        return carry

    lax.fori_loop(0, heads, head_norm, 0, unroll=min(4, heads))

    def up(s):
        return remote(acts.at[s], acts.at[s], a_s.at[0, s], a_r.at[s], c + 2, t)

    def down(s):
        return remote(acts.at[s], acts.at[s], a_s.at[1, s], a_r.at[s], c - 2, t)

    def across(s):
        return remote(acts.at[s], acts.at[s], a_s.at[2, s], a_r.at[s], c + 1 - 2 * j, t)

    def state_copy(to):
        return remote(shares.at[to], state, st_s.at[to], st_r, to, t)

    @pl.when(z < chips - 1)
    def _():
        up(c).start()

    @pl.when(z > 0)
    def _():
        down(c).start()

    across(c).start()

    @pl.when(c == last)
    def _():
        for to in range(last):
            state_copy(to).start()
        state[...] = shares[last]

    def chip_at(i):
        near_end = jnp.minimum(z, chips - 1 - z)
        half = (i + 1) // 2
        near = jnp.where(i % 2 == 1, z - half, z + half)
        far = jnp.where(z < chips - 1 - z, z + (i - near_end), z - (i - near_end))
        return jnp.where(i <= 2 * near_end, near, far)

    def project(s):
        depth = w.shape[1]
        for n in range(0, depth, 256):
            m = min(n + 256, depth)
            parts[s, :, n:m] = dot(acts[s], w[:, n:m], ((1,), (0,))).astype(BF16)
        for off in range(1, groups):
            to = (t + off) % groups
            src = parts.at[s, pl.ds(pl.multiple_of(to * rows_here, rows_here), rows_here)]
            remote(src, arrived.at[s, off - 1], rs_s.at[s], rs_r.at[s], c, to).start()

    own_rows = pl.ds(pl.multiple_of(t * rows_here, rows_here), rows_here)
    home = c // ratio

    def final_copy(s):
        return remote(
            summed.at[s], layer.at[c % ratio, own_rows], fin_s.at[s], fin_r, s, home
        )

    def stays(s):
        return jnp.logical_and(s == c, home == t)

    def finish(s):
        wait_bytes(arrived.at[s], rs_r.at[s])
        added = parts[s, own_rows].astype(F32)
        for off in range(1, groups):
            added = added + arrived[s, off - 1].astype(F32)
        summed[s] = added.astype(BF16)

        @pl.when(stays(s))
        def _():
            pltpu.make_async_copy(summed.at[s], layer.at[c % ratio, own_rows], fin_r).start()

        @pl.when(jnp.logical_not(stays(s)))
        def _():
            final_copy(s).start()

    w_copy.wait()

    def step(i, carry):
        zk = chip_at(i)
        s = 2 * zk + j

        @pl.when(i > 0)
        def _():
            wait_bytes(acts.at[s], a_r.at[s])

            @pl.when(jnp.logical_and(zk < z, z < chips - 1))
            def _():
                up(s).start()

            @pl.when(jnp.logical_and(zk > z, z > 0))
            def _():
                down(s).start()

            across(s).start()

        project(s)
        other = 2 * zk + 1 - j
        wait_bytes(acts.at[other], a_r.at[other])
        project(other)

        @pl.when(i > 0)
        def _():
            before = chip_at(i - 1)
            finish(2 * before + j)
            finish(2 * before + 1 - j)

        return carry

    lax.fori_loop(0, chips, step, 0)
    final_chip = chip_at(chips - 1)
    finish(2 * final_chip + j)
    finish(2 * final_chip + 1 - j)

    wait_bytes(layer, fin_r)
    wait_bytes(ssq_in, sq_s)

    @pl.when(c < last)
    def _():
        wait_bytes(state, st_r)
        for g in range(chunks):
            chain_copy(g).wait_send()

    @pl.when(c == last)
    def _():
        for to in range(last):
            state_copy(to).wait_send()

    def drain_chip(zk, carry):
        s = 2 * zk + j

        @pl.when(jnp.logical_and(zk <= z, z < chips - 1))
        def _():
            up(s).wait_send()

        @pl.when(jnp.logical_and(zk >= z, z > 0))
        def _():
            down(s).wait_send()

        across(s).wait_send()
        return carry

    lax.fori_loop(0, chips, drain_chip, 0)

    def drain_slot(s, carry):
        wait_bytes(arrived.at[s], rs_s.at[s])

        @pl.when(jnp.logical_not(stays(s)))
        def _():
            final_copy(s).wait_send()

        return carry

    lax.fori_loop(0, peers, drain_slot, 0)


def per_device(peers, groups, queries, keys, values, log_keep, state_in, norm_gain, out_weight):
    heads, tokens = log_keep.shape
    width = state_in.shape[1]
    columns = queries.shape[1]
    depth = out_weight.shape[1]
    chunks = min(4, heads)
    share = width // peers
    ratio = peers // groups
    rows_here = tokens // groups
    dma = pltpu.SemaphoreType.DMA
    vmem = pl.BlockSpec(memory_space=pltpu.VMEM)
    normed, state, layer = pl.pallas_call(
        functools.partial(kernel, peers, groups, chunks),
        out_shape=(
            jax.ShapeDtypeStruct((tokens, columns), BF16),
            jax.ShapeDtypeStruct((heads * share, width), F32),
            jax.ShapeDtypeStruct((ratio, tokens, depth), BF16),
        ),
        in_specs=[vmem] * 6 + [pl.BlockSpec(memory_space=pl.ANY)],
        out_specs=(vmem, vmem, vmem),
        scratch_shapes=[
            pltpu.VMEM(out_weight.shape, BF16),
            pltpu.VMEM((128, tokens), F32),
            pltpu.VMEM((128, tokens), F32),
            pltpu.VMEM((tokens, 128), F32),
            pltpu.VMEM((heads, width, width), F32),
            pltpu.VMEM((heads, width, width), F32),
            pltpu.VMEM((tokens, columns), F32),
            pltpu.VMEM((heads, width, width), BF16),
            pltpu.VMEM((heads, width, width), BF16),
            pltpu.VMEM((peers, heads * share, width), F32),
            pltpu.VMEM((8, tokens), F32),
            pltpu.VMEM((groups - 1, 8, tokens), F32),
            pltpu.VMEM((peers, tokens, columns), BF16),
            pltpu.VMEM((peers, tokens, depth), BF16),
            pltpu.VMEM((peers, groups - 1, rows_here, depth), BF16),
            pltpu.VMEM((peers, rows_here, depth), BF16),
            dma,
            dma((chunks,)),
            dma((chunks,)),
            dma((peers,)),
            dma,
            dma,
            dma,
            dma((3, peers)),
            dma((peers,)),
            dma((peers,)),
            dma((peers,)),
            dma((peers,)),
            dma,
        ],
        compiler_params=pltpu.CompilerParams(
            collective_id=0, has_side_effects=True, vmem_limit_bytes=56 * 1024 * 1024
        ),
        name="attend_project",
    )(queries, keys, values, log_keep, state_in, norm_gain[None, :], out_weight)
    state = state.reshape(heads, share, width)
    layer = layer.transpose(1, 0, 2).reshape(tokens, ratio * depth)
    return normed, state, layer


def solution(mesh):
    peers, groups = mesh.shape["ctx"], mesh.shape["tp"]
    return jax.shard_map(
        functools.partial(per_device, peers, groups),
        mesh=mesh,
        in_specs=(
            P("ctx", "tp"),
            P("ctx", "tp"),
            P("ctx", "tp"),
            P("tp", "ctx"),
            P("tp", None, None),
            P("tp"),
            P("tp", "ctx"),
        ),
        out_specs=(P("ctx", "tp"), P("tp", "ctx", None), P("ctx", "tp")),
        check_vma=False,
    )
```

```python
import functools

import jax
import jax.numpy as jnp
from jax import lax
from jax.experimental import pallas as pl
from jax.experimental.pallas import tpu as pltpu
from jax.sharding import PartitionSpec as P

EPSILON = 1e-06
HIGH = lax.Precision.HIGHEST
MESH = pl.DeviceIdType.MESH
F32 = jnp.float32
BF16 = jnp.bfloat16


def wait_bytes(ref, sem):
    pltpu.make_async_copy(ref, ref, sem).wait()


def dot(a, b, over, precision=None):
    return lax.dot_general(
        a, b, (over, ((), ())), precision=precision, preferred_element_type=F32
    )


def kernel(
    peers, groups, chunks,
    q, k, v, logs, s_in, gain, w_hbm,
    normed, state, layer,
    w, padded, brow, bcol, inc, zst, att, cin, cout, shares, ssq_out, ssq_in,
    acts, parts, arrived, summed, squares, scale, landed,
    w_sem, chain_s, chain_r, st_s, st_r, sq_s, sq_r, a_s, a_r, rs_s, rs_r, fin_s, fin_r,
):
    c = lax.axis_index("ctx")
    t = lax.axis_index("tp")
    heads, tokens = logs.shape
    width = s_in.shape[1]
    share = state.shape[0] // heads
    chips = peers // 2
    z, j = c // 2, c % 2
    ratio = peers // groups
    rows_here = tokens // groups
    per_chunk = heads // chunks
    last = peers - 1

    def remote(src, dst, send, recv, ctx, tp):
        return pltpu.make_async_remote_copy(
            src_ref=src, dst_ref=dst, send_sem=send, recv_sem=recv,
            device_id={"ctx": ctx, "tp": tp}, device_id_type=MESH,
        )

    w_copy = pltpu.make_async_copy(w_hbm, w, w_sem)
    w_copy.start()
    barrier = pltpu.get_barrier_semaphore()
    everyone = peers * groups

    def greet(i, carry):
        other = (c * groups + t + i) % everyone
        pl.semaphore_signal(
            barrier, inc=1,
            device_id={"ctx": other // groups, "tp": other % groups},
            device_id_type=MESH,
        )
        return carry

    lax.fori_loop(1, everyone, greet, 0)

    padded[...] = jnp.zeros_like(padded)
    padded[0:heads, :] = logs[...]
    rows = lax.broadcasted_iota(jnp.int32, (tokens, tokens), 0)
    cols = lax.broadcasted_iota(jnp.int32, (tokens, tokens), 1)
    upper = jnp.where(rows <= cols, 1.0, 0.0).astype(F32)
    by_row = dot(padded[...], upper, ((1,), (0,)), HIGH)
    brow[...] = by_row
    bcol[...] = by_row.T
    lane = lax.broadcasted_iota(jnp.int32, (tokens, 128), 1)

    def column(h):
        return jnp.sum(jnp.where(lane == h, bcol[...], 0.0), axis=1, keepdims=True)

    def head_cols(h):
        return pl.ds(pl.multiple_of(h * width, width), width)

    def head_increment(h, carry):
        hs = head_cols(h)
        summed_logs = column(h)
        factor = jnp.exp(summed_logs[tokens - 1 : tokens] - summed_logs)
        decayed = (k[:, hs].astype(F32) * factor).astype(BF16)
        inc[h] = dot(decayed, v[:, hs], ((0,), (0,)))
        return carry

    lax.fori_loop(0, heads, head_increment, 0, unroll=min(4, heads))
    pl.semaphore_wait(barrier, everyone - 1)

    def chain_copy(g):
        part = pl.ds(g * per_chunk, per_chunk)
        return remote(cout.at[part], cin.at[part], chain_s.at[g], chain_r.at[g], c + 1, t)

    def pass_on(g, incoming):
        for h in range(g * per_chunk, (g + 1) * per_chunk):
            start = incoming[h].astype(F32)
            zst[h] = start
            end = jnp.exp(brow[h : h + 1, tokens - 1 : tokens]) * start + inc[h]
            cout[h] = end.astype(BF16)

            @pl.when(c == last)
            def _():
                for to in range(peers):
                    shares[to, h * share : (h + 1) * share, :] = end[to * share : (to + 1) * share]

        @pl.when(c < last)
        def _():
            chain_copy(g).start()

    @pl.when(c == 0)
    def _():
        for g in range(chunks):
            pass_on(g, s_in)

    causal = rows >= cols

    def head_intra(h, carry):
        hs = head_cols(h)
        scores = dot(q[:, hs], k[:, hs], ((1,), (1,)))
        spread = jnp.minimum(column(h) - brow[pl.ds(h, 1), :], 0.0)
        weights = (scores * jnp.where(causal, jnp.exp(spread), 0.0)).astype(BF16)
        att[:, hs] = dot(weights, v[:, hs], ((1,), (0,)))
        return carry

    lax.fori_loop(0, heads, head_intra, 0, unroll=min(2, heads))

    @pl.when(c > 0)
    def _():
        for g in range(chunks):
            wait_bytes(cin.at[pl.ds(g * per_chunk, per_chunk)], chain_r.at[g])
            pass_on(g, cin)

    def up(s, g):
        return remote(acts.at[s, g], acts.at[s, g], a_s.at[0, s, g], a_r.at[s, g], c + 2, t)

    def down(s, g):
        return remote(acts.at[s, g], acts.at[s, g], a_s.at[1, s, g], a_r.at[s, g], c - 2, t)

    def across(s, g):
        return remote(
            acts.at[s, g], acts.at[s, g], a_s.at[2, s, g], a_r.at[s, g], c + 1 - 2 * j, t
        )

    def state_copy(to):
        return remote(shares.at[to], state, st_s.at[to], st_r, to, t)

    squares[...] = jnp.zeros_like(squares)
    for g in range(chunks):
        for i in range(per_chunk):
            h = g * per_chunk + i
            hs = slice(h * width, (h + 1) * width)
            inter = dot(q[:, hs], zst[h].astype(BF16), ((1,), (0,))) * jnp.exp(bcol[:, h : h + 1])
            whole = att[:, hs] + inter
            att[:, hs] = whole
            squares[...] += whole * whole
            acts[c, g, :, i * width : (i + 1) * width] = (whole * gain[:, hs]).astype(BF16)

        @pl.when(z > 0)
        def _():
            down(c, g).start()

        across(c, g).start()

    @pl.when(z < chips - 1)
    def _():
        for g in range(chunks):
            up(c, g).start()

    ssq_out[...] = dot(jnp.ones((8, width), F32), squares[...], ((1,), (1,)), HIGH)
    for off in range(1, groups):
        remote(ssq_out, ssq_in.at[off - 1], sq_s, sq_r, c, (t + off) % groups).start()

    @pl.when(c == last)
    def _():
        for to in range(last):
            state_copy(to).start()
        state[...] = shares[last]

    wait_bytes(ssq_in, sq_r)
    total = ssq_out[...]
    for off in range(1, groups):
        total = total + ssq_in[off - 1]
    spread_total = dot(total, jnp.full((8, width), 0.125, F32), ((0,), (0,)), HIGH)
    scale[...] = lax.rsqrt(spread_total / (groups * heads * width) + EPSILON)

    def head_norm(h, carry):
        hs = head_cols(h)
        normed[:, hs] = (att[:, hs] * scale[...] * gain[:, hs]).astype(BF16)
        return carry

    lax.fori_loop(0, heads, head_norm, 0, unroll=min(4, heads))

    def chip_at(i):
        near_end = jnp.minimum(z, chips - 1 - z)
        half = (i + 1) // 2
        near = jnp.where(i % 2 == 1, z - half, z + half)
        far = jnp.where(z < chips - 1 - z, z + (i - near_end), z - (i - near_end))
        return jnp.where(i <= 2 * near_end, near, far)

    def project(s):
        depth = w.shape[1]
        rows_of = jnp.concatenate([acts[s, g] for g in range(chunks)], axis=1)
        for n in range(0, depth, 256):
            m = min(n + 256, depth)
            parts[s, :, n:m] = dot(rows_of, w[:, n:m], ((1,), (0,))).astype(BF16)
        for off in range(1, groups):
            to = (t + off) % groups
            src = parts.at[s, pl.ds(pl.multiple_of(to * rows_here, rows_here), rows_here)]
            remote(src, arrived.at[s, off - 1], rs_s.at[s], rs_r.at[s], c, to).start()

    own_rows = pl.ds(pl.multiple_of(t * rows_here, rows_here), rows_here)
    home = c // ratio

    def final_copy(s):
        return remote(
            summed.at[s], landed.at[c % ratio, own_rows], fin_s.at[s], fin_r, s, home
        )

    def stays(s):
        return jnp.logical_and(s == c, home == t)

    def finish(s):
        wait_bytes(arrived.at[s], rs_r.at[s])
        added = parts[s, own_rows].astype(F32)
        for off in range(1, groups):
            added = added + arrived[s, off - 1].astype(F32)
        summed[s] = added.astype(BF16)

        @pl.when(stays(s))
        def _():
            pltpu.make_async_copy(summed.at[s], landed.at[c % ratio, own_rows], fin_r).start()

        @pl.when(jnp.logical_not(stays(s)))
        def _():
            final_copy(s).start()

    w_copy.wait()

    def step(i, carry):
        zk = chip_at(i)
        s = 2 * zk + j

        @pl.when(i > 0)
        def _():
            for g in range(chunks):
                wait_bytes(acts.at[s, g], a_r.at[s, g])

                @pl.when(jnp.logical_and(zk < z, z < chips - 1))
                def _():
                    up(s, g).start()

                @pl.when(jnp.logical_and(zk > z, z > 0))
                def _():
                    down(s, g).start()

                across(s, g).start()

        project(s)
        other = 2 * zk + 1 - j
        for g in range(chunks):
            wait_bytes(acts.at[other, g], a_r.at[other, g])
        project(other)

        @pl.when(i > 0)
        def _():
            before = chip_at(i - 1)
            finish(2 * before + j)
            finish(2 * before + 1 - j)

        return carry

    lax.fori_loop(0, chips, step, 0)
    final_chip = chip_at(chips - 1)
    finish(2 * final_chip + j)
    finish(2 * final_chip + 1 - j)

    wait_bytes(landed, fin_r)
    depth = w.shape[1]
    for i in range(ratio):
        for n in range(0, depth, 128):
            m = min(n + 128, depth)
            out = (landed[i, :, n:m].astype(F32) * scale[:, 0 : m - n]).astype(BF16)
            if depth % 128 == 0:
                layer[:, i * depth + n : i * depth + m] = out
            else:
                layer[i, :, n:m] = out
    wait_bytes(ssq_in, sq_s)

    @pl.when(c < last)
    def _():
        wait_bytes(state, st_r)
        for g in range(chunks):
            chain_copy(g).wait_send()

    @pl.when(c == last)
    def _():
        for to in range(last):
            state_copy(to).wait_send()

    def drain_chip(zk, carry):
        s = 2 * zk + j

        @pl.when(jnp.logical_and(zk <= z, z < chips - 1))
        def _():
            for g in range(chunks):
                up(s, g).wait_send()

        @pl.when(jnp.logical_and(zk >= z, z > 0))
        def _():
            for g in range(chunks):
                down(s, g).wait_send()

        for g in range(chunks):
            across(s, g).wait_send()
        return carry

    lax.fori_loop(0, chips, drain_chip, 0)

    def drain_slot(s, carry):
        wait_bytes(arrived.at[s], rs_s.at[s])

        @pl.when(jnp.logical_not(stays(s)))
        def _():
            final_copy(s).wait_send()

        return carry

    lax.fori_loop(0, peers, drain_slot, 0)


def per_device(peers, groups, queries, keys, values, log_keep, state_in, norm_gain, out_weight):
    heads, tokens = log_keep.shape
    width = state_in.shape[1]
    columns = queries.shape[1]
    depth = out_weight.shape[1]
    chunks = min(4, heads)
    share = width // peers
    ratio = peers // groups
    rows_here = tokens // groups
    dma = pltpu.SemaphoreType.DMA
    vmem = pl.BlockSpec(memory_space=pltpu.VMEM)
    normed, state, layer = pl.pallas_call(
        functools.partial(kernel, peers, groups, chunks),
        out_shape=(
            jax.ShapeDtypeStruct((tokens, columns), BF16),
            jax.ShapeDtypeStruct((heads * share, width), F32),
            jax.ShapeDtypeStruct(
                (tokens, ratio * depth) if depth % 128 == 0 else (ratio, tokens, depth), BF16
            ),
        ),
        in_specs=[vmem] * 6 + [pl.BlockSpec(memory_space=pl.ANY)],
        out_specs=(vmem, vmem, vmem),
        scratch_shapes=[
            pltpu.VMEM(out_weight.shape, BF16),
            pltpu.VMEM((128, tokens), F32),
            pltpu.VMEM((128, tokens), F32),
            pltpu.VMEM((tokens, 128), F32),
            pltpu.VMEM((heads, width, width), F32),
            pltpu.VMEM((heads, width, width), F32),
            pltpu.VMEM((tokens, columns), F32),
            pltpu.VMEM((heads, width, width), BF16),
            pltpu.VMEM((heads, width, width), BF16),
            pltpu.VMEM((peers, heads * share, width), F32),
            pltpu.VMEM((8, tokens), F32),
            pltpu.VMEM((groups - 1, 8, tokens), F32),
            pltpu.VMEM((peers, chunks, tokens, columns // chunks), BF16),
            pltpu.VMEM((peers, tokens, depth), BF16),
            pltpu.VMEM((peers, groups - 1, rows_here, depth), BF16),
            pltpu.VMEM((peers, rows_here, depth), BF16),
            pltpu.VMEM((tokens, width), F32),
            pltpu.VMEM((tokens, width), F32),
            pltpu.VMEM((ratio, tokens, depth), BF16),
            dma,
            dma((chunks,)),
            dma((chunks,)),
            dma((peers,)),
            dma,
            dma,
            dma,
            dma((3, peers, chunks)),
            dma((peers, chunks)),
            dma((peers,)),
            dma((peers,)),
            dma((peers,)),
            dma,
        ],
        compiler_params=pltpu.CompilerParams(
            collective_id=0, has_side_effects=True, vmem_limit_bytes=56 * 1024 * 1024
        ),
        name="attend_project",
    )(queries, keys, values, log_keep, state_in, norm_gain[None, :], out_weight)
    state = state.reshape(heads, share, width)
    if layer.ndim == 3:
        layer = layer.transpose(1, 0, 2).reshape(tokens, ratio * depth)
    return normed, state, layer


def solution(mesh):
    peers, groups = mesh.shape["ctx"], mesh.shape["tp"]
    return jax.shard_map(
        functools.partial(per_device, peers, groups),
        mesh=mesh,
        in_specs=(
            P("ctx", "tp"),
            P("ctx", "tp"),
            P("ctx", "tp"),
            P("tp", "ctx"),
            P("tp", None, None),
            P("tp"),
            P("tp", "ctx"),
        ),
        out_specs=(P("ctx", "tp"), P("tp", "ctx", None), P("ctx", "tp")),
        check_vma=False,
    )
```

```python
import functools

import jax
import jax.numpy as jnp
from jax import lax
from jax.experimental import pallas as pl
from jax.experimental.pallas import tpu as pltpu
from jax.sharding import PartitionSpec as P

EPSILON = 1e-06
HIGH = lax.Precision.HIGHEST
MESH = pl.DeviceIdType.MESH
F32 = jnp.float32
BF16 = jnp.bfloat16


def wait_bytes(ref, sem):
    pltpu.make_async_copy(ref, ref, sem).wait()


def dot(a, b, over, precision=None):
    return lax.dot_general(
        a, b, (over, ((), ())), precision=precision, preferred_element_type=F32
    )


def kernel(
    peers, groups, chunks,
    q, k, v, logs, s_in, gain, w_hbm,
    normed, state, layer,
    w, padded, brow, bcol, inc, zst, att, cin, cout, shares, ssq_out, ssq_in,
    acts, parts, arrived, summed, squares, scale, landed, relay,
    w_sem, chain_s, chain_r, st_s, st_r, sq_s, sq_r, a_s, a_r, rs_s, rs_r, fin_s, mid_r, fwd_s, fin_r,
):
    c = lax.axis_index("ctx")
    t = lax.axis_index("tp")
    heads, tokens = logs.shape
    width = s_in.shape[1]
    share = state.shape[0] // heads
    chips = peers // 2
    z, j = c // 2, c % 2
    ratio = peers // groups
    rows_here = tokens // groups
    per_chunk = heads // chunks
    last = peers - 1

    def remote(src, dst, send, recv, ctx, tp):
        return pltpu.make_async_remote_copy(
            src_ref=src, dst_ref=dst, send_sem=send, recv_sem=recv,
            device_id={"ctx": ctx, "tp": tp}, device_id_type=MESH,
        )

    w_copy = pltpu.make_async_copy(w_hbm, w, w_sem)
    w_copy.start()
    barrier = pltpu.get_barrier_semaphore()
    everyone = peers * groups

    def greet(i, carry):
        other = (c * groups + t + i) % everyone
        pl.semaphore_signal(
            barrier, inc=1,
            device_id={"ctx": other // groups, "tp": other % groups},
            device_id_type=MESH,
        )
        return carry

    lax.fori_loop(1, everyone, greet, 0)

    padded[...] = jnp.zeros_like(padded)
    padded[0:heads, :] = logs[...]
    rows = lax.broadcasted_iota(jnp.int32, (tokens, tokens), 0)
    cols = lax.broadcasted_iota(jnp.int32, (tokens, tokens), 1)
    upper = jnp.where(rows <= cols, 1.0, 0.0).astype(F32)
    by_row = dot(padded[...], upper, ((1,), (0,)), HIGH)
    brow[...] = by_row
    bcol[...] = by_row.T
    lane = lax.broadcasted_iota(jnp.int32, (tokens, 128), 1)

    def column(h):
        return jnp.sum(jnp.where(lane == h, bcol[...], 0.0), axis=1, keepdims=True)

    def head_cols(h):
        return pl.ds(pl.multiple_of(h * width, width), width)

    def head_increment(h, carry):
        hs = head_cols(h)
        summed_logs = column(h)
        factor = jnp.exp(summed_logs[tokens - 1 : tokens] - summed_logs)
        decayed = (k[:, hs].astype(F32) * factor).astype(BF16)
        inc[h] = dot(decayed, v[:, hs], ((0,), (0,)))
        return carry

    lax.fori_loop(0, heads, head_increment, 0, unroll=min(4, heads))
    pl.semaphore_wait(barrier, everyone - 1)

    def chain_copy(g):
        part = pl.ds(g * per_chunk, per_chunk)
        return remote(cout.at[part], cin.at[part], chain_s.at[g], chain_r.at[g], c + 1, t)

    def pass_on(g, incoming):
        for h in range(g * per_chunk, (g + 1) * per_chunk):
            start = incoming[h].astype(F32)
            zst[h] = start
            end = jnp.exp(brow[h : h + 1, tokens - 1 : tokens]) * start + inc[h]
            cout[h] = end.astype(BF16)

            @pl.when(c == last)
            def _():
                for to in range(peers):
                    shares[to, h * share : (h + 1) * share, :] = end[to * share : (to + 1) * share]

        @pl.when(c < last)
        def _():
            chain_copy(g).start()

    @pl.when(c == 0)
    def _():
        for g in range(chunks):
            pass_on(g, s_in)

    causal = rows >= cols

    def head_intra(h, carry):
        hs = head_cols(h)
        scores = dot(q[:, hs], k[:, hs], ((1,), (1,)))
        spread = jnp.minimum(column(h) - brow[pl.ds(h, 1), :], 0.0)
        weights = (scores * jnp.where(causal, jnp.exp(spread), 0.0)).astype(BF16)
        att[:, hs] = dot(weights, v[:, hs], ((1,), (0,)))
        return carry

    lax.fori_loop(0, heads, head_intra, 0, unroll=min(2, heads))

    @pl.when(c > 0)
    def _():
        for g in range(chunks):
            wait_bytes(cin.at[pl.ds(g * per_chunk, per_chunk)], chain_r.at[g])
            pass_on(g, cin)

    def up(s, g):
        return remote(acts.at[s, g], acts.at[s, g], a_s.at[0, s, g], a_r.at[s, g], c + 2, t)

    def down(s, g):
        return remote(acts.at[s, g], acts.at[s, g], a_s.at[1, s, g], a_r.at[s, g], c - 2, t)

    def across(s, g):
        return remote(
            acts.at[s, g], acts.at[s, g], a_s.at[2, s, g], a_r.at[s, g], c + 1 - 2 * j, t
        )

    def state_copy(to):
        return remote(shares.at[to], state, st_s.at[to], st_r, to, t)

    squares[...] = jnp.zeros_like(squares)
    for g in range(chunks):
        for i in range(per_chunk):
            h = g * per_chunk + i
            hs = slice(h * width, (h + 1) * width)
            inter = dot(q[:, hs], zst[h].astype(BF16), ((1,), (0,))) * jnp.exp(bcol[:, h : h + 1])
            whole = att[:, hs] + inter
            att[:, hs] = whole
            squares[...] += whole * whole
            acts[c, g, :, i * width : (i + 1) * width] = (whole * gain[:, hs]).astype(BF16)

        @pl.when(z > 0)
        def _():
            down(c, g).start()

        across(c, g).start()

    @pl.when(z < chips - 1)
    def _():
        for g in range(chunks):
            up(c, g).start()

    ssq_out[...] = dot(jnp.ones((8, width), F32), squares[...], ((1,), (1,)), HIGH)
    for off in range(1, groups):
        remote(ssq_out, ssq_in.at[off - 1], sq_s, sq_r, c, (t + off) % groups).start()

    @pl.when(c == last)
    def _():
        for to in range(last):
            state_copy(to).start()
        state[...] = shares[last]

    wait_bytes(ssq_in, sq_r)
    total = ssq_out[...]
    for off in range(1, groups):
        total = total + ssq_in[off - 1]
    spread_total = dot(total, jnp.full((8, width), 0.125, F32), ((0,), (0,)), HIGH)
    scale[...] = lax.rsqrt(spread_total / (groups * heads * width) + EPSILON)

    def head_norm(h, carry):
        hs = head_cols(h)
        normed[:, hs] = (att[:, hs] * scale[...] * gain[:, hs]).astype(BF16)
        return carry

    lax.fori_loop(0, heads, head_norm, 0, unroll=min(4, heads))

    def chip_at(i):
        near_end = jnp.minimum(z, chips - 1 - z)
        half = (i + 1) // 2
        near = jnp.where(i % 2 == 1, z - half, z + half)
        far = jnp.where(z < chips - 1 - z, z + (i - near_end), z - (i - near_end))
        return jnp.where(i <= 2 * near_end, near, far)

    def project(s):
        depth = w.shape[1]
        rows_of = jnp.concatenate([acts[s, g] for g in range(chunks)], axis=1)
        for n in range(0, depth, 256):
            m = min(n + 256, depth)
            parts[s, :, n:m] = dot(rows_of, w[:, n:m], ((1,), (0,))).astype(BF16)
        for off in range(1, groups):
            to = (t + off) % groups
            src = parts.at[s, pl.ds(pl.multiple_of(to * rows_here, rows_here), rows_here)]
            remote(src, arrived.at[s, off - 1], rs_s.at[s], rs_r.at[s], c, to).start()

    own_rows = pl.ds(pl.multiple_of(t * rows_here, rows_here), rows_here)

    def to_owner(s):
        return remote(summed.at[s], relay.at[c], fin_s.at[s], mid_r.at[c], s, t)

    def finish(s):
        wait_bytes(arrived.at[s], rs_r.at[s])
        added = parts[s, own_rows].astype(F32)
        for off in range(1, groups):
            added = added + arrived[s, off - 1].astype(F32)

        @pl.when(s == c)
        def _():
            relay[c] = added.astype(BF16)

        @pl.when(s != c)
        def _():
            summed[s] = added.astype(BF16)
            to_owner(s).start()

    def to_home(frm):
        return remote(
            relay.at[frm], landed.at[frm % ratio, own_rows], fwd_s.at[frm], fin_r, c, frm // ratio
        )

    def deliver(frm):
        @pl.when(frm != c)
        def _():
            wait_bytes(relay.at[frm], mid_r.at[frm])

        @pl.when(frm // ratio == t)
        def _():
            pltpu.make_async_copy(relay.at[frm], landed.at[frm % ratio, own_rows], fin_r).start()

        @pl.when(frm // ratio != t)
        def _():
            to_home(frm).start()

    early = chips <= 4

    w_copy.wait()

    def step(i, carry):
        zk = chip_at(i)
        s = 2 * zk + j

        @pl.when(i > 0)
        def _():
            for g in range(chunks):
                wait_bytes(acts.at[s, g], a_r.at[s, g])

                @pl.when(jnp.logical_and(zk < z, z < chips - 1))
                def _():
                    up(s, g).start()

                @pl.when(jnp.logical_and(zk > z, z > 0))
                def _():
                    down(s, g).start()

                across(s, g).start()
                if g == 0:
                    before = chip_at(i - 1)
                    finish(2 * before + j)
                    finish(2 * before + 1 - j)
                    if early:

                        @pl.when(i > 1)
                        def _():
                            twice = chip_at(i - 2)
                            deliver(2 * twice + j)
                            deliver(2 * twice + 1 - j)

        project(s)
        other = 2 * zk + 1 - j
        for g in range(chunks):
            wait_bytes(acts.at[other, g], a_r.at[other, g])
        project(other)
        return carry

    lax.fori_loop(0, chips, step, 0)
    final_chip = chip_at(chips - 1)
    finish(2 * final_chip + j)
    finish(2 * final_chip + 1 - j)

    def deliver_chip(i, carry):
        zk = chip_at(i)
        deliver(2 * zk + j)
        deliver(2 * zk + 1 - j)
        return carry

    lax.fori_loop(max(0, chips - 2) if early else 0, chips, deliver_chip, 0)

    wait_bytes(landed, fin_r)
    depth = w.shape[1]
    for i in range(ratio):
        for n in range(0, depth, 128):
            m = min(n + 128, depth)
            out = (landed[i, :, n:m].astype(F32) * scale[:, 0 : m - n]).astype(BF16)
            if depth % 128 == 0:
                layer[:, i * depth + n : i * depth + m] = out
            else:
                layer[i, :, n:m] = out
    wait_bytes(ssq_in, sq_s)

    @pl.when(c < last)
    def _():
        wait_bytes(state, st_r)
        for g in range(chunks):
            chain_copy(g).wait_send()

    @pl.when(c == last)
    def _():
        for to in range(last):
            state_copy(to).wait_send()

    def drain_chip(zk, carry):
        s = 2 * zk + j

        @pl.when(jnp.logical_and(zk <= z, z < chips - 1))
        def _():
            for g in range(chunks):
                up(s, g).wait_send()

        @pl.when(jnp.logical_and(zk >= z, z > 0))
        def _():
            for g in range(chunks):
                down(s, g).wait_send()

        for g in range(chunks):
            across(s, g).wait_send()
        return carry

    lax.fori_loop(0, chips, drain_chip, 0)

    def drain_slot(s, carry):
        wait_bytes(arrived.at[s], rs_s.at[s])

        @pl.when(s != c)
        def _():
            to_owner(s).wait_send()

        @pl.when(s // ratio != t)
        def _():
            to_home(s).wait_send()

        return carry

    lax.fori_loop(0, peers, drain_slot, 0)


def per_device(peers, groups, queries, keys, values, log_keep, state_in, norm_gain, out_weight):
    heads, tokens = log_keep.shape
    width = state_in.shape[1]
    columns = queries.shape[1]
    depth = out_weight.shape[1]
    chunks = min(4, heads)
    share = width // peers
    ratio = peers // groups
    rows_here = tokens // groups
    dma = pltpu.SemaphoreType.DMA
    vmem = pl.BlockSpec(memory_space=pltpu.VMEM)
    normed, state, layer = pl.pallas_call(
        functools.partial(kernel, peers, groups, chunks),
        out_shape=(
            jax.ShapeDtypeStruct((tokens, columns), BF16),
            jax.ShapeDtypeStruct((heads * share, width), F32),
            jax.ShapeDtypeStruct(
                (tokens, ratio * depth) if depth % 128 == 0 else (ratio, tokens, depth), BF16
            ),
        ),
        in_specs=[vmem] * 6 + [pl.BlockSpec(memory_space=pl.ANY)],
        out_specs=(vmem, vmem, vmem),
        scratch_shapes=[
            pltpu.VMEM(out_weight.shape, BF16),
            pltpu.VMEM((128, tokens), F32),
            pltpu.VMEM((128, tokens), F32),
            pltpu.VMEM((tokens, 128), F32),
            pltpu.VMEM((heads, width, width), F32),
            pltpu.VMEM((heads, width, width), F32),
            pltpu.VMEM((tokens, columns), F32),
            pltpu.VMEM((heads, width, width), BF16),
            pltpu.VMEM((heads, width, width), BF16),
            pltpu.VMEM((peers, heads * share, width), F32),
            pltpu.VMEM((8, tokens), F32),
            pltpu.VMEM((groups - 1, 8, tokens), F32),
            pltpu.VMEM((peers, chunks, tokens, columns // chunks), BF16),
            pltpu.VMEM((peers, tokens, depth), BF16),
            pltpu.VMEM((peers, groups - 1, rows_here, depth), BF16),
            pltpu.VMEM((peers, rows_here, depth), BF16),
            pltpu.VMEM((tokens, width), F32),
            pltpu.VMEM((tokens, width), F32),
            pltpu.VMEM((ratio, tokens, depth), BF16),
            pltpu.VMEM((peers, rows_here, depth), BF16),
            dma,
            dma((chunks,)),
            dma((chunks,)),
            dma((peers,)),
            dma,
            dma,
            dma,
            dma((3, peers, chunks)),
            dma((peers, chunks)),
            dma((peers,)),
            dma((peers,)),
            dma((peers,)),
            dma((peers,)),
            dma((peers,)),
            dma,
        ],
        compiler_params=pltpu.CompilerParams(
            collective_id=0, has_side_effects=True, vmem_limit_bytes=56 * 1024 * 1024
        ),
        name="attend_project",
    )(queries, keys, values, log_keep, state_in, norm_gain[None, :], out_weight)
    if layer.ndim == 3:
        layer = layer.transpose(1, 0, 2).reshape(tokens, ratio * depth)
    normed, state, layer = write_out(normed, state, layer)
    return normed, state.reshape(heads, share, width), layer


def write_out(*results):
    def body(*refs):
        for src, dst in zip(refs[: len(results)], refs[len(results) :]):
            dst[...] = src[...]

    steps = 4 if all(r.shape[0] % 64 == 0 for r in results) else 2
    specs = [pl.BlockSpec((r.shape[0] // steps, r.shape[1]), lambda i: (i, 0)) for r in results]
    return pl.pallas_call(
        body,
        grid=(steps,),
        out_shape=[jax.ShapeDtypeStruct(r.shape, r.dtype) for r in results],
        in_specs=specs,
        out_specs=specs,
        name="write_out",
    )(*results)


def solution(mesh):
    peers, groups = mesh.shape["ctx"], mesh.shape["tp"]
    return jax.shard_map(
        functools.partial(per_device, peers, groups),
        mesh=mesh,
        in_specs=(
            P("ctx", "tp"),
            P("ctx", "tp"),
            P("ctx", "tp"),
            P("tp", "ctx"),
            P("tp", None, None),
            P("tp"),
            P("tp", "ctx"),
        ),
        out_specs=(P("ctx", "tp"), P("tp", "ctx", None), P("ctx", "tp")),
        check_vma=False,
    )
```

```python
import functools

import jax
import jax.numpy as jnp
from jax import lax
from jax.experimental import pallas as pl
from jax.experimental.pallas import tpu as pltpu
from jax.sharding import PartitionSpec as P

EPSILON = 1e-06
HIGH = lax.Precision.HIGHEST
MESH = pl.DeviceIdType.MESH
F32 = jnp.float32
BF16 = jnp.bfloat16


def wait_bytes(ref, sem):
    pltpu.make_async_copy(ref, ref, sem).wait()


def dot(a, b, over, precision=None):
    return lax.dot_general(
        a, b, (over, ((), ())), precision=precision, preferred_element_type=F32
    )


def kernel(
    peers, groups, chunks,
    q, k, v, logs, s_in, gain, w_hbm,
    normed, state, layer,
    w, padded, brow, bcol, inc, zst, att, cin, cout, shares, ssq_out, ssq_in,
    acts, parts, arrived, summed, squares, scale, landed, relay,
    w_extra, parts_x, arrived_x, summed_x, relay_x,
    w_sem, chain_s, chain_r, st_s, st_r, sq_s, sq_r, a_s, a_r, rs_s, rs_r, fin_s, mid_r, fwd_s, fin_r,
    wx_s, wx_r, rsx_s, rsx_r, finx_s, midx_r,
):
    c = lax.axis_index("ctx")
    t = lax.axis_index("tp")
    heads, tokens = logs.shape
    width = s_in.shape[1]
    share = state.shape[0] // heads
    chips = peers // 2
    z, j = c // 2, c % 2
    ratio = peers // groups
    rows_here = tokens // groups
    per_chunk = heads // chunks
    last = peers - 1

    split = chips >= 4 and chunks % 2 == 0
    kept = chunks // 2
    half = w.shape[0] // 2
    at_end = jnp.logical_or(z == 0, z == chips - 1)
    beside_end = jnp.logical_or(z == 1, z == chips - 2)
    near_end_chip = jnp.where(z == 1, 0, chips - 1)
    helped = 2 * near_end_chip + j

    def apart(a, b):
        return jnp.logical_or(a - b >= 2, b - a >= 2)

    def far(zk):
        return jnp.logical_and(at_end, apart(zk, z))

    def beyond(zk):
        return jnp.logical_and(beside_end, apart(zk, near_end_chip))

    def goes(g, zk):
        return jnp.logical_not(far(zk)) if split and g >= kept else True

    def goes_up(g, zk):
        limit = chips - 2 if split and g >= kept else chips - 1
        return jnp.logical_and(zk < z, z < limit)

    def goes_down(g, zk):
        limit = 1 if split and g >= kept else 0
        return jnp.logical_and(zk > z, z > limit)

    def remote(src, dst, send, recv, ctx, tp):
        return pltpu.make_async_remote_copy(
            src_ref=src, dst_ref=dst, send_sem=send, recv_sem=recv,
            device_id={"ctx": ctx, "tp": tp}, device_id_type=MESH,
        )

    w_copy = pltpu.make_async_copy(w_hbm, w, w_sem)
    w_copy.start()
    barrier = pltpu.get_barrier_semaphore()
    everyone = peers * groups

    def greet(i, carry):
        other = (c * groups + t + i) % everyone
        pl.semaphore_signal(
            barrier, inc=1,
            device_id={"ctx": other // groups, "tp": other % groups},
            device_id_type=MESH,
        )
        return carry

    lax.fori_loop(1, everyone, greet, 0)

    padded[...] = jnp.zeros_like(padded)
    padded[0:heads, :] = logs[...]
    rows = lax.broadcasted_iota(jnp.int32, (tokens, tokens), 0)
    cols = lax.broadcasted_iota(jnp.int32, (tokens, tokens), 1)
    upper = jnp.where(rows <= cols, 1.0, 0.0).astype(F32)
    by_row = dot(padded[...], upper, ((1,), (0,)), HIGH)
    brow[...] = by_row
    bcol[...] = by_row.T
    lane = lax.broadcasted_iota(jnp.int32, (tokens, 128), 1)

    def column(h):
        return jnp.sum(jnp.where(lane == h, bcol[...], 0.0), axis=1, keepdims=True)

    def head_cols(h):
        return pl.ds(pl.multiple_of(h * width, width), width)

    def head_increment(h, carry):
        hs = head_cols(h)
        summed_logs = column(h)
        factor = jnp.exp(summed_logs[tokens - 1 : tokens] - summed_logs)
        decayed = (k[:, hs].astype(F32) * factor).astype(BF16)
        inc[h] = dot(decayed, v[:, hs], ((0,), (0,)))
        return carry

    lax.fori_loop(0, heads, head_increment, 0, unroll=min(4, heads))
    pl.semaphore_wait(barrier, everyone - 1)

    def hand_over():
        return remote(
            w_hbm.at[pl.ds(half, half)], w_extra, wx_s, wx_r, jnp.where(z == 0, c + 2, c - 2), t
        )

    if split:

        @pl.when(z == chips - 1)
        def _():
            hand_over().start()

    def chain_copy(g):
        part = pl.ds(g * per_chunk, per_chunk)
        return remote(cout.at[part], cin.at[part], chain_s.at[g], chain_r.at[g], c + 1, t)

    def pass_on(g, incoming):
        for h in range(g * per_chunk, (g + 1) * per_chunk):
            start = incoming[h].astype(F32)
            zst[h] = start
            end = jnp.exp(brow[h : h + 1, tokens - 1 : tokens]) * start + inc[h]
            cout[h] = end.astype(BF16)

            @pl.when(c == last)
            def _():
                for to in range(peers):
                    shares[to, h * share : (h + 1) * share, :] = end[to * share : (to + 1) * share]

        @pl.when(c < last)
        def _():
            chain_copy(g).start()

    @pl.when(c == 0)
    def _():
        for g in range(chunks):
            pass_on(g, s_in)

    causal = rows >= cols

    def head_intra(h, carry):
        hs = head_cols(h)
        scores = dot(q[:, hs], k[:, hs], ((1,), (1,)))
        spread = jnp.minimum(column(h) - brow[pl.ds(h, 1), :], 0.0)
        weights = (scores * jnp.where(causal, jnp.exp(spread), 0.0)).astype(BF16)
        att[:, hs] = dot(weights, v[:, hs], ((1,), (0,)))
        return carry

    lax.fori_loop(0, heads, head_intra, 0, unroll=min(2, heads))

    @pl.when(c > 0)
    def _():
        for g in range(chunks):
            wait_bytes(cin.at[pl.ds(g * per_chunk, per_chunk)], chain_r.at[g])
            pass_on(g, cin)

    def up(s, g):
        return remote(acts.at[s, g], acts.at[s, g], a_s.at[0, s, g], a_r.at[s, g], c + 2, t)

    def down(s, g):
        return remote(acts.at[s, g], acts.at[s, g], a_s.at[1, s, g], a_r.at[s, g], c - 2, t)

    def across(s, g):
        return remote(
            acts.at[s, g], acts.at[s, g], a_s.at[2, s, g], a_r.at[s, g], c + 1 - 2 * j, t
        )

    def state_copy(to):
        return remote(shares.at[to], state, st_s.at[to], st_r, to, t)

    squares[...] = jnp.zeros_like(squares)
    for g in range(chunks):
        for i in range(per_chunk):
            h = g * per_chunk + i
            hs = slice(h * width, (h + 1) * width)
            inter = dot(q[:, hs], zst[h].astype(BF16), ((1,), (0,))) * jnp.exp(bcol[:, h : h + 1])
            whole = att[:, hs] + inter
            att[:, hs] = whole
            squares[...] += whole * whole
            acts[c, g, :, i * width : (i + 1) * width] = (whole * gain[:, hs]).astype(BF16)

        @pl.when(z > 0)
        def _():
            down(c, g).start()

        across(c, g).start()

    @pl.when(z < chips - 1)
    def _():
        for g in range(chunks):
            up(c, g).start()

    if split:

        @pl.when(z == 0)
        def _():
            hand_over().start()

    ssq_out[...] = dot(jnp.ones((8, width), F32), squares[...], ((1,), (1,)), HIGH)
    for off in range(1, groups):
        remote(ssq_out, ssq_in.at[off - 1], sq_s, sq_r, c, (t + off) % groups).start()

    @pl.when(c == last)
    def _():
        for to in range(last):
            state_copy(to).start()
        state[...] = shares[last]

    wait_bytes(ssq_in, sq_r)
    total = ssq_out[...]
    for off in range(1, groups):
        total = total + ssq_in[off - 1]
    spread_total = dot(total, jnp.full((8, width), 0.125, F32), ((0,), (0,)), HIGH)
    scale[...] = lax.rsqrt(spread_total / (groups * heads * width) + EPSILON)

    def head_norm(h, carry):
        hs = head_cols(h)
        normed[:, hs] = (att[:, hs] * scale[...] * gain[:, hs]).astype(BF16)
        return carry

    lax.fori_loop(0, heads, head_norm, 0, unroll=min(4, heads))

    def chip_at(i):
        near_end = jnp.minimum(z, chips - 1 - z)
        half = (i + 1) // 2
        near = jnp.where(i % 2 == 1, z - half, z + half)
        far = jnp.where(z < chips - 1 - z, z + (i - near_end), z - (i - near_end))
        return jnp.where(i <= 2 * near_end, near, far)

    depth = w.shape[1]

    def multiply(s, first, end, weights, rows_used, out):
        rows_of = jnp.concatenate([acts[s, g] for g in range(first, end)], axis=1)
        for n in range(0, depth, 256):
            m = min(n + 256, depth)
            out[s, :, n:m] = dot(rows_of, weights[0:rows_used, n:m], ((1,), (0,))).astype(BF16)

    def scatter(s, out, into, send, recv):
        for off in range(1, groups):
            to = (t + off) % groups
            src = out.at[s, pl.ds(pl.multiple_of(to * rows_here, rows_here), rows_here)]
            remote(src, into.at[s, off - 1], send.at[s], recv.at[s], c, to).start()

    def project(s, zk):
        if split:

            @pl.when(far(zk))
            def _():
                multiply(s, 0, kept, w, half, parts)

            @pl.when(jnp.logical_not(far(zk)))
            def _():
                multiply(s, 0, chunks, w, 2 * half, parts)

        else:
            multiply(s, 0, chunks, w, 2 * half, parts)
        scatter(s, parts, arrived, rs_s, rs_r)

    def project_extra(s):
        multiply(s, kept, chunks, w_extra, half, parts_x)
        scatter(s, parts_x, arrived_x, rsx_s, rsx_r)

    own_rows = pl.ds(pl.multiple_of(t * rows_here, rows_here), rows_here)

    def to_owner(s):
        return remote(summed.at[s], relay.at[c], fin_s.at[s], mid_r.at[c], s, t)

    def gathered_sum(s, out, into, recv):
        wait_bytes(into.at[s], recv.at[s])
        added = out[s, own_rows].astype(F32)
        for off in range(1, groups):
            added = added + into[s, off - 1].astype(F32)
        return added

    def extra_to_owner(s):
        return remote(
            summed_x.at[s], relay_x.at[helped], finx_s.at[s], midx_r.at[helped], s, t
        )

    def finish_extra(s):
        summed_x[s] = gathered_sum(s, parts_x, arrived_x, rsx_r).astype(BF16)
        extra_to_owner(s).start()

    def finish(s):
        added = gathered_sum(s, parts, arrived, rs_r)

        @pl.when(s == c)
        def _():
            relay[c] = added.astype(BF16)

        @pl.when(s != c)
        def _():
            summed[s] = added.astype(BF16)
            to_owner(s).start()

    def to_home(frm):
        return remote(
            relay.at[frm], landed.at[frm % ratio, own_rows], fwd_s.at[frm], fin_r, c, frm // ratio
        )

    def deliver(frm):
        @pl.when(frm != c)
        def _():
            wait_bytes(relay.at[frm], mid_r.at[frm])

        if split:
            source = frm // 2
            from_end = jnp.logical_or(source == 0, source == chips - 1)

            @pl.when(jnp.logical_and(from_end, apart(source, z)))
            def _():
                wait_bytes(relay_x.at[frm], midx_r.at[frm])
                both = relay[frm].astype(F32) + relay_x[frm].astype(F32)
                relay[frm] = both.astype(BF16)

        @pl.when(frm // ratio == t)
        def _():
            pltpu.make_async_copy(relay.at[frm], landed.at[frm % ratio, own_rows], fin_r).start()

        @pl.when(frm // ratio != t)
        def _():
            to_home(frm).start()

    early = chips <= 4

    w_copy.wait()

    def step(i, carry):
        zk = chip_at(i)
        s = 2 * zk + j

        @pl.when(i > 0)
        def _():
            for g in range(chunks):

                @pl.when(goes(g, zk))
                def _():
                    wait_bytes(acts.at[s, g], a_r.at[s, g])
                    across(s, g).start()

                @pl.when(goes_up(g, zk))
                def _():
                    up(s, g).start()

                @pl.when(goes_down(g, zk))
                def _():
                    down(s, g).start()

                if g == 0:
                    before = chip_at(i - 1)
                    finish(2 * before + j)
                    finish(2 * before + 1 - j)
                    if early:

                        @pl.when(i > 1)
                        def _():
                            twice = chip_at(i - 2)
                            deliver(2 * twice + j)
                            deliver(2 * twice + 1 - j)

        project(s, zk)
        other = 2 * zk + 1 - j
        for g in range(chunks):

            @pl.when(goes(g, zk))
            def _():
                wait_bytes(acts.at[other, g], a_r.at[other, g])

        project(other, zk)
        return carry

    lax.fori_loop(0, chips, step, 0)
    if split:

        @pl.when(beside_end)
        def _():
            wait_bytes(w_extra, wx_r)

        def extra_chip(zk, carry):
            @pl.when(beyond(zk))
            def _():
                project_extra(2 * zk)
                project_extra(2 * zk + 1)

            return carry

        lax.fori_loop(0, chips, extra_chip, 0)

    final_chip = chip_at(chips - 1)
    finish(2 * final_chip + j)
    finish(2 * final_chip + 1 - j)
    if split:

        def extra_sums(zk, carry):
            @pl.when(beyond(zk))
            def _():
                finish_extra(2 * zk)
                finish_extra(2 * zk + 1)

            return carry

        lax.fori_loop(0, chips, extra_sums, 0)

    def deliver_chip(i, carry):
        zk = chip_at(i)
        deliver(2 * zk + j)
        deliver(2 * zk + 1 - j)
        return carry

    lax.fori_loop(max(0, chips - 2) if early else 0, chips, deliver_chip, 0)

    wait_bytes(landed, fin_r)
    for i in range(ratio):
        for n in range(0, depth, 128):
            m = min(n + 128, depth)
            out = (landed[i, :, n:m].astype(F32) * scale[:, 0 : m - n]).astype(BF16)
            if depth % 128 == 0:
                layer[:, i * depth + n : i * depth + m] = out
            else:
                layer[i, :, n:m] = out
    wait_bytes(ssq_in, sq_s)

    @pl.when(c < last)
    def _():
        wait_bytes(state, st_r)
        for g in range(chunks):
            chain_copy(g).wait_send()

    @pl.when(c == last)
    def _():
        for to in range(last):
            state_copy(to).wait_send()

    def drain_chip(zk, carry):
        s = 2 * zk + j

        for g in range(chunks):

            @pl.when(jnp.logical_or(goes_up(g, zk), jnp.logical_and(zk == z, z < chips - 1)))
            def _():
                up(s, g).wait_send()

            @pl.when(jnp.logical_or(goes_down(g, zk), jnp.logical_and(zk == z, z > 0)))
            def _():
                down(s, g).wait_send()

            @pl.when(goes(g, zk))
            def _():
                across(s, g).wait_send()

        if split:

            @pl.when(beyond(zk))
            def _():
                for x in (2 * zk, 2 * zk + 1):
                    wait_bytes(arrived_x.at[x], rsx_s.at[x])
                    extra_to_owner(x).wait_send()

        return carry

    if split:

        @pl.when(at_end)
        def _():
            hand_over().wait_send()

    lax.fori_loop(0, chips, drain_chip, 0)

    def drain_slot(s, carry):
        wait_bytes(arrived.at[s], rs_s.at[s])

        @pl.when(s != c)
        def _():
            to_owner(s).wait_send()

        @pl.when(s // ratio != t)
        def _():
            to_home(s).wait_send()

        return carry

    lax.fori_loop(0, peers, drain_slot, 0)


def per_device(peers, groups, queries, keys, values, log_keep, state_in, norm_gain, out_weight):
    heads, tokens = log_keep.shape
    width = state_in.shape[1]
    columns = queries.shape[1]
    depth = out_weight.shape[1]
    chunks = min(4, heads)
    share = width // peers
    ratio = peers // groups
    rows_here = tokens // groups
    dma = pltpu.SemaphoreType.DMA
    vmem = pl.BlockSpec(memory_space=pltpu.VMEM)
    normed, state, layer = pl.pallas_call(
        functools.partial(kernel, peers, groups, chunks),
        out_shape=(
            jax.ShapeDtypeStruct((tokens, columns), BF16),
            jax.ShapeDtypeStruct((heads * share, width), F32),
            jax.ShapeDtypeStruct(
                (tokens, ratio * depth) if depth % 128 == 0 else (ratio, tokens, depth), BF16
            ),
        ),
        in_specs=[vmem] * 6 + [pl.BlockSpec(memory_space=pl.ANY)],
        out_specs=(vmem, vmem, vmem),
        scratch_shapes=[
            pltpu.VMEM(out_weight.shape, BF16),
            pltpu.VMEM((128, tokens), F32),
            pltpu.VMEM((128, tokens), F32),
            pltpu.VMEM((tokens, 128), F32),
            pltpu.VMEM((heads, width, width), F32),
            pltpu.VMEM((heads, width, width), F32),
            pltpu.VMEM((tokens, columns), F32),
            pltpu.VMEM((heads, width, width), BF16),
            pltpu.VMEM((heads, width, width), BF16),
            pltpu.VMEM((peers, heads * share, width), F32),
            pltpu.VMEM((8, tokens), F32),
            pltpu.VMEM((groups - 1, 8, tokens), F32),
            pltpu.VMEM((peers, chunks, tokens, columns // chunks), BF16),
            pltpu.VMEM((peers, tokens, depth), BF16),
            pltpu.VMEM((peers, groups - 1, rows_here, depth), BF16),
            pltpu.VMEM((peers, rows_here, depth), BF16),
            pltpu.VMEM((tokens, width), F32),
            pltpu.VMEM((tokens, width), F32),
            pltpu.VMEM((ratio, tokens, depth), BF16),
            pltpu.VMEM((peers, rows_here, depth), BF16),
            pltpu.VMEM((columns // 2, depth), BF16),
            pltpu.VMEM((peers, tokens, depth), BF16),
            pltpu.VMEM((peers, groups - 1, rows_here, depth), BF16),
            pltpu.VMEM((peers, rows_here, depth), BF16),
            pltpu.VMEM((peers, rows_here, depth), BF16),
            dma,
            dma((chunks,)),
            dma((chunks,)),
            dma((peers,)),
            dma,
            dma,
            dma,
            dma((3, peers, chunks)),
            dma((peers, chunks)),
            dma((peers,)),
            dma((peers,)),
            dma((peers,)),
            dma((peers,)),
            dma((peers,)),
            dma,
            dma,
            dma,
            dma((peers,)),
            dma((peers,)),
            dma((peers,)),
            dma((peers,)),
        ],
        compiler_params=pltpu.CompilerParams(
            collective_id=0, has_side_effects=True, vmem_limit_bytes=56 * 1024 * 1024
        ),
        name="attend_project",
    )(queries, keys, values, log_keep, state_in, norm_gain[None, :], out_weight)
    if layer.ndim == 3:
        layer = layer.transpose(1, 0, 2).reshape(tokens, ratio * depth)
    normed, state, layer = write_out(normed, state, layer)
    return normed, state.reshape(heads, share, width), layer


def write_out(*results):
    def body(*refs):
        for src, dst in zip(refs[: len(results)], refs[len(results) :]):
            dst[...] = src[...]

    steps = 4 if all(r.shape[0] % 64 == 0 for r in results) else 2
    specs = [pl.BlockSpec((r.shape[0] // steps, r.shape[1]), lambda i: (i, 0)) for r in results]
    return pl.pallas_call(
        body,
        grid=(steps,),
        out_shape=[jax.ShapeDtypeStruct(r.shape, r.dtype) for r in results],
        in_specs=specs,
        out_specs=specs,
        name="write_out",
    )(*results)


def solution(mesh):
    peers, groups = mesh.shape["ctx"], mesh.shape["tp"]
    return jax.shard_map(
        functools.partial(per_device, peers, groups),
        mesh=mesh,
        in_specs=(
            P("ctx", "tp"),
            P("ctx", "tp"),
            P("ctx", "tp"),
            P("tp", "ctx"),
            P("tp", None, None),
            P("tp"),
            P("tp", "ctx"),
        ),
        out_specs=(P("ctx", "tp"), P("tp", "ctx", None), P("ctx", "tp")),
        check_vma=False,
    )
```

```python
import functools

import jax
import jax.numpy as jnp
from jax import lax
from jax.experimental import pallas as pl
from jax.experimental.pallas import tpu as pltpu
from jax.sharding import PartitionSpec as P

EPSILON = 1e-06
HIGH = lax.Precision.HIGHEST
MESH = pl.DeviceIdType.MESH
F32 = jnp.float32
BF16 = jnp.bfloat16


def wait_bytes(ref, sem):
    pltpu.make_async_copy(ref, ref, sem).wait()


def dot(a, b, over, precision=None):
    return lax.dot_general(
        a, b, (over, ((), ())), precision=precision, preferred_element_type=F32
    )


def kernel(
    peers, groups, chunks,
    q, k, v, logs, s_in, gain, w_hbm,
    normed, state, layer,
    w, padded, brow, bcol, inc, zst, att, cin, cout, shares, ssq_out, ssq_in,
    acts, parts, arrived, summed, squares, scale, landed, relay,
    w_extra, parts_x, arrived_x, summed_x, relay_x,
    w_sem, chain_s, chain_r, st_s, st_r, sq_s, sq_r, a_s, a_r, rs_s, rs_r, fin_s, mid_r, fwd_s, fin_r,
    wx_s, wx_r, rsx_s, rsx_r, finx_s, midx_r,
):
    c = lax.axis_index("ctx")
    t = lax.axis_index("tp")
    heads, tokens = logs.shape
    width = s_in.shape[1]
    share = state.shape[0] // heads
    chips = peers // 2
    z, j = c // 2, c % 2
    ratio = peers // groups
    rows_here = tokens // groups
    per_chunk = heads // chunks
    last = peers - 1

    split = chips >= 4 and chunks % 2 == 0
    kept = chunks // 2
    half = w.shape[0] // 2
    at_end = jnp.logical_or(z == 0, z == chips - 1)
    beside_end = jnp.logical_or(z == 1, z == chips - 2)
    near_end_chip = jnp.where(z == 1, 0, chips - 1)
    helped = 2 * near_end_chip + j

    def apart(a, b):
        return jnp.logical_or(a - b >= 2, b - a >= 2)

    def far(zk):
        return jnp.logical_and(at_end, apart(zk, z))

    def beyond(zk):
        return jnp.logical_and(beside_end, apart(zk, near_end_chip))

    def goes(g, zk):
        return jnp.logical_not(far(zk)) if split and g >= kept else True

    def goes_up(g, zk):
        limit = chips - 2 if split and g >= kept else chips - 1
        return jnp.logical_and(zk < z, z < limit)

    def goes_down(g, zk):
        limit = 1 if split and g >= kept else 0
        return jnp.logical_and(zk > z, z > limit)

    def remote(src, dst, send, recv, ctx, tp):
        return pltpu.make_async_remote_copy(
            src_ref=src, dst_ref=dst, send_sem=send, recv_sem=recv,
            device_id={"ctx": ctx, "tp": tp}, device_id_type=MESH,
        )

    w_copy = pltpu.make_async_copy(w_hbm, w, w_sem)
    w_copy.start()
    barrier = pltpu.get_barrier_semaphore()
    everyone = peers * groups

    def greet(i, carry):
        other = (c * groups + t + i) % everyone
        pl.semaphore_signal(
            barrier, inc=1,
            device_id={"ctx": other // groups, "tp": other % groups},
            device_id_type=MESH,
        )
        return carry

    lax.fori_loop(1, everyone, greet, 0)

    padded[...] = jnp.zeros_like(padded)
    padded[0:heads, :] = logs[...]
    rows = lax.broadcasted_iota(jnp.int32, (tokens, tokens), 0)
    cols = lax.broadcasted_iota(jnp.int32, (tokens, tokens), 1)
    upper = jnp.where(rows <= cols, 1.0, 0.0).astype(F32)
    by_row = dot(padded[...], upper, ((1,), (0,)), HIGH)
    brow[...] = by_row
    bcol[...] = by_row.T
    lane = lax.broadcasted_iota(jnp.int32, (tokens, 128), 1)

    def column(h):
        return jnp.sum(jnp.where(lane == h, bcol[...], 0.0), axis=1, keepdims=True)

    def head_cols(h):
        return pl.ds(pl.multiple_of(h * width, width), width)

    def head_increment(h, carry):
        hs = head_cols(h)
        summed_logs = column(h)
        factor = jnp.exp(summed_logs[tokens - 1 : tokens] - summed_logs)
        decayed = (k[:, hs].astype(F32) * factor).astype(BF16)
        inc[h] = dot(decayed, v[:, hs], ((0,), (0,)))
        return carry

    lax.fori_loop(0, heads, head_increment, 0, unroll=min(4, heads))
    pl.semaphore_wait(barrier, everyone - 1)

    def hand_over():
        return remote(
            w_hbm.at[pl.ds(half, half)], w_extra, wx_s, wx_r, jnp.where(z == 0, c + 2, c - 2), t
        )

    if split:

        @pl.when(z == chips - 1)
        def _():
            hand_over().start()

    def chain_copy(g):
        part = pl.ds(g * per_chunk, per_chunk)
        return remote(cout.at[part], cin.at[part], chain_s.at[g], chain_r.at[g], c + 1, t)

    def pass_on(g, incoming):
        for h in range(g * per_chunk, (g + 1) * per_chunk):
            start = incoming[h].astype(F32)
            zst[h] = start
            end = jnp.exp(brow[h : h + 1, tokens - 1 : tokens]) * start + inc[h]
            cout[h] = end.astype(BF16)

            @pl.when(c == last)
            def _():
                for to in range(peers):
                    shares[to, h * share : (h + 1) * share, :] = end[to * share : (to + 1) * share]

        @pl.when(c < last)
        def _():
            chain_copy(g).start()

    @pl.when(c == 0)
    def _():
        for g in range(chunks):
            pass_on(g, s_in)

    causal = rows >= cols

    def head_intra(h, carry):
        hs = head_cols(h)
        scores = dot(q[:, hs], k[:, hs], ((1,), (1,)))
        spread = jnp.minimum(column(h) - brow[pl.ds(h, 1), :], 0.0)
        weights = (scores * jnp.where(causal, jnp.exp(spread), 0.0)).astype(BF16)
        att[:, hs] = dot(weights, v[:, hs], ((1,), (0,)))
        return carry

    def intra(g):
        lax.fori_loop(
            g * per_chunk, (g + 1) * per_chunk, head_intra, 0, unroll=min(4, per_chunk)
        )

    sooner = z < chips // 2

    @pl.when(sooner)
    def _():
        intra(0)

    @pl.when(jnp.logical_not(sooner))
    def _():
        lax.fori_loop(0, heads, head_intra, 0, unroll=min(4, heads))

    @pl.when(c > 0)
    def _():
        for g in range(chunks):
            wait_bytes(cin.at[pl.ds(g * per_chunk, per_chunk)], chain_r.at[g])
            pass_on(g, cin)

    def up(s, g):
        return remote(acts.at[s, g], acts.at[s, g], a_s.at[0, s, g], a_r.at[s, g], c + 2, t)

    def down(s, g):
        return remote(acts.at[s, g], acts.at[s, g], a_s.at[1, s, g], a_r.at[s, g], c - 2, t)

    def across(s, g):
        return remote(
            acts.at[s, g], acts.at[s, g], a_s.at[2, s, g], a_r.at[s, g], c + 1 - 2 * j, t
        )

    def state_copy(to):
        return remote(shares.at[to], state, st_s.at[to], st_r, to, t)

    squares[...] = jnp.zeros_like(squares)
    for g in range(chunks):
        if g > 0:

            @pl.when(sooner)
            def _():
                intra(g)

        for i in range(per_chunk):
            h = g * per_chunk + i
            hs = slice(h * width, (h + 1) * width)
            inter = dot(q[:, hs], zst[h].astype(BF16), ((1,), (0,))) * jnp.exp(bcol[:, h : h + 1])
            whole = att[:, hs] + inter
            att[:, hs] = whole
            squares[...] += whole * whole
            acts[c, g, :, i * width : (i + 1) * width] = (whole * gain[:, hs]).astype(BF16)

        @pl.when(z > 0)
        def _():
            down(c, g).start()

        @pl.when(z == 0)
        def _():
            up(c, g).start()

        across(c, g).start()

    @pl.when(jnp.logical_and(z > 0, z < chips - 1))
    def _():
        for g in range(chunks):
            up(c, g).start()

    ssq_out[...] = dot(jnp.ones((8, width), F32), squares[...], ((1,), (1,)), HIGH)
    for off in range(1, groups):
        remote(ssq_out, ssq_in.at[off - 1], sq_s, sq_r, c, (t + off) % groups).start()

    @pl.when(c == last)
    def _():
        for to in range(last):
            state_copy(to).start()
        state[...] = shares[last]

    wait_bytes(ssq_in, sq_r)
    total = ssq_out[...]
    for off in range(1, groups):
        total = total + ssq_in[off - 1]
    spread_total = dot(total, jnp.full((8, width), 0.125, F32), ((0,), (0,)), HIGH)
    scale[...] = lax.rsqrt(spread_total / (groups * heads * width) + EPSILON)

    def head_norm(h, carry):
        hs = head_cols(h)
        normed[:, hs] = (att[:, hs] * scale[...] * gain[:, hs]).astype(BF16)
        return carry

    lax.fori_loop(0, heads, head_norm, 0, unroll=min(4, heads))

    def chip_at(i):
        near_end = jnp.minimum(z, chips - 1 - z)
        half = (i + 1) // 2
        near = jnp.where(i % 2 == 1, z - half, z + half)
        far = jnp.where(z < chips - 1 - z, z + (i - near_end), z - (i - near_end))
        return jnp.where(i <= 2 * near_end, near, far)

    depth = w.shape[1]

    def multiply(s, first, end, weights, rows_used, out):
        rows_of = jnp.concatenate([acts[s, g] for g in range(first, end)], axis=1)
        for n in range(0, depth, 256):
            m = min(n + 256, depth)
            out[s, :, n:m] = dot(rows_of, weights[0:rows_used, n:m], ((1,), (0,))).astype(BF16)

    def scatter(s, out, into, send, recv):
        for off in range(1, groups):
            to = (t + off) % groups
            src = out.at[s, pl.ds(pl.multiple_of(to * rows_here, rows_here), rows_here)]
            remote(src, into.at[s, off - 1], send.at[s], recv.at[s], c, to).start()

    def project(s, zk):
        if split:

            @pl.when(far(zk))
            def _():
                multiply(s, 0, kept, w, half, parts)

            @pl.when(jnp.logical_not(far(zk)))
            def _():
                multiply(s, 0, chunks, w, 2 * half, parts)

        else:
            multiply(s, 0, chunks, w, 2 * half, parts)
        scatter(s, parts, arrived, rs_s, rs_r)

    def project_extra(s):
        multiply(s, kept, chunks, w_extra, half, parts_x)
        scatter(s, parts_x, arrived_x, rsx_s, rsx_r)

    own_rows = pl.ds(pl.multiple_of(t * rows_here, rows_here), rows_here)

    def to_owner(s):
        return remote(summed.at[s], relay.at[c], fin_s.at[s], mid_r.at[c], s, t)

    def gathered_sum(s, out, into, recv):
        wait_bytes(into.at[s], recv.at[s])
        added = out[s, own_rows].astype(F32)
        for off in range(1, groups):
            added = added + into[s, off - 1].astype(F32)
        return added

    def extra_to_owner(s):
        return remote(
            summed_x.at[s], relay_x.at[helped], finx_s.at[s], midx_r.at[helped], s, t
        )

    def finish_extra(s):
        summed_x[s] = gathered_sum(s, parts_x, arrived_x, rsx_r).astype(BF16)
        extra_to_owner(s).start()

    def finish(s):
        added = gathered_sum(s, parts, arrived, rs_r)

        @pl.when(s == c)
        def _():
            relay[c] = added.astype(BF16)

        @pl.when(s != c)
        def _():
            summed[s] = added.astype(BF16)
            to_owner(s).start()

    def to_home(frm):
        return remote(
            relay.at[frm], landed.at[frm % ratio, own_rows], fwd_s.at[frm], fin_r, c, frm // ratio
        )

    def deliver(frm):
        @pl.when(frm != c)
        def _():
            wait_bytes(relay.at[frm], mid_r.at[frm])

        if split:
            source = frm // 2
            from_end = jnp.logical_or(source == 0, source == chips - 1)

            @pl.when(jnp.logical_and(from_end, apart(source, z)))
            def _():
                wait_bytes(relay_x.at[frm], midx_r.at[frm])
                both = relay[frm].astype(F32) + relay_x[frm].astype(F32)
                relay[frm] = both.astype(BF16)

        @pl.when(frm // ratio == t)
        def _():
            pltpu.make_async_copy(relay.at[frm], landed.at[frm % ratio, own_rows], fin_r).start()

        @pl.when(frm // ratio != t)
        def _():
            to_home(frm).start()

    early = chips <= 4

    w_copy.wait()

    if split:

        @pl.when(z == 0)
        def _():
            for g in range(chunks):
                up(c, g).wait_send()
            hand_over().start()

    def step(i, carry):
        zk = chip_at(i)
        s = 2 * zk + j

        @pl.when(i > 0)
        def _():
            for g in range(chunks):

                @pl.when(goes(g, zk))
                def _():
                    wait_bytes(acts.at[s, g], a_r.at[s, g])
                    across(s, g).start()

                @pl.when(goes_up(g, zk))
                def _():
                    up(s, g).start()

                @pl.when(goes_down(g, zk))
                def _():
                    down(s, g).start()

                if g == 0:
                    before = chip_at(i - 1)
                    finish(2 * before + j)
                    finish(2 * before + 1 - j)
                    if early:

                        @pl.when(i > 1)
                        def _():
                            twice = chip_at(i - 2)
                            deliver(2 * twice + j)
                            deliver(2 * twice + 1 - j)

        project(s, zk)
        other = 2 * zk + 1 - j
        for g in range(chunks):

            @pl.when(goes(g, zk))
            def _():
                wait_bytes(acts.at[other, g], a_r.at[other, g])

        project(other, zk)
        return carry

    lax.fori_loop(0, chips, step, 0)
    if split:

        @pl.when(beside_end)
        def _():
            wait_bytes(w_extra, wx_r)

        def extra_chip(zk, carry):
            @pl.when(beyond(zk))
            def _():
                project_extra(2 * zk)
                project_extra(2 * zk + 1)

            return carry

        lax.fori_loop(0, chips, extra_chip, 0)

    final_chip = chip_at(chips - 1)
    finish(2 * final_chip + j)
    finish(2 * final_chip + 1 - j)
    if split:

        def extra_sums(zk, carry):
            @pl.when(beyond(zk))
            def _():
                finish_extra(2 * zk)
                finish_extra(2 * zk + 1)

            return carry

        lax.fori_loop(0, chips, extra_sums, 0)

    def deliver_chip(i, carry):
        zk = chip_at(i)
        deliver(2 * zk + j)
        deliver(2 * zk + 1 - j)
        return carry

    lax.fori_loop(max(0, chips - 2) if early else 0, chips, deliver_chip, 0)

    wait_bytes(landed, fin_r)
    for i in range(ratio):
        for n in range(0, depth, 128):
            m = min(n + 128, depth)
            out = (landed[i, :, n:m].astype(F32) * scale[:, 0 : m - n]).astype(BF16)
            if depth % 128 == 0:
                layer[:, i * depth + n : i * depth + m] = out
            else:
                layer[i, :, n:m] = out
    wait_bytes(ssq_in, sq_s)

    @pl.when(c < last)
    def _():
        wait_bytes(state, st_r)
        for g in range(chunks):
            chain_copy(g).wait_send()

    @pl.when(c == last)
    def _():
        for to in range(last):
            state_copy(to).wait_send()

    def drain_chip(zk, carry):
        s = 2 * zk + j

        for g in range(chunks):

            waited = 0 if split else -1

            @pl.when(
                jnp.logical_or(
                    goes_up(g, zk),
                    jnp.logical_and(zk == z, jnp.logical_and(z > waited, z < chips - 1)),
                )
            )
            def _():
                up(s, g).wait_send()

            @pl.when(jnp.logical_or(goes_down(g, zk), jnp.logical_and(zk == z, z > 0)))
            def _():
                down(s, g).wait_send()

            @pl.when(goes(g, zk))
            def _():
                across(s, g).wait_send()

        if split:

            @pl.when(beyond(zk))
            def _():
                for x in (2 * zk, 2 * zk + 1):
                    wait_bytes(arrived_x.at[x], rsx_s.at[x])
                    extra_to_owner(x).wait_send()

        return carry

    if split:

        @pl.when(at_end)
        def _():
            hand_over().wait_send()

    lax.fori_loop(0, chips, drain_chip, 0)

    def drain_slot(s, carry):
        wait_bytes(arrived.at[s], rs_s.at[s])

        @pl.when(s != c)
        def _():
            to_owner(s).wait_send()

        @pl.when(s // ratio != t)
        def _():
            to_home(s).wait_send()

        return carry

    lax.fori_loop(0, peers, drain_slot, 0)


def per_device(peers, groups, queries, keys, values, log_keep, state_in, norm_gain, out_weight):
    heads, tokens = log_keep.shape
    width = state_in.shape[1]
    columns = queries.shape[1]
    depth = out_weight.shape[1]
    chunks = min(4, heads)
    share = width // peers
    ratio = peers // groups
    rows_here = tokens // groups
    dma = pltpu.SemaphoreType.DMA
    vmem = pl.BlockSpec(memory_space=pltpu.VMEM)
    normed, state, layer = pl.pallas_call(
        functools.partial(kernel, peers, groups, chunks),
        out_shape=(
            jax.ShapeDtypeStruct((tokens, columns), BF16),
            jax.ShapeDtypeStruct((heads * share, width), F32),
            jax.ShapeDtypeStruct(
                (tokens, ratio * depth) if depth % 128 == 0 else (ratio, tokens, depth), BF16
            ),
        ),
        in_specs=[vmem] * 6 + [pl.BlockSpec(memory_space=pl.ANY)],
        out_specs=(vmem, vmem, vmem),
        scratch_shapes=[
            pltpu.VMEM(out_weight.shape, BF16),
            pltpu.VMEM((128, tokens), F32),
            pltpu.VMEM((128, tokens), F32),
            pltpu.VMEM((tokens, 128), F32),
            pltpu.VMEM((heads, width, width), F32),
            pltpu.VMEM((heads, width, width), F32),
            pltpu.VMEM((tokens, columns), F32),
            pltpu.VMEM((heads, width, width), BF16),
            pltpu.VMEM((heads, width, width), BF16),
            pltpu.VMEM((peers, heads * share, width), F32),
            pltpu.VMEM((8, tokens), F32),
            pltpu.VMEM((groups - 1, 8, tokens), F32),
            pltpu.VMEM((peers, chunks, tokens, columns // chunks), BF16),
            pltpu.VMEM((peers, tokens, depth), BF16),
            pltpu.VMEM((peers, groups - 1, rows_here, depth), BF16),
            pltpu.VMEM((peers, rows_here, depth), BF16),
            pltpu.VMEM((tokens, width), F32),
            pltpu.VMEM((tokens, width), F32),
            pltpu.VMEM((ratio, tokens, depth), BF16),
            pltpu.VMEM((peers, rows_here, depth), BF16),
            pltpu.VMEM((columns // 2, depth), BF16),
            pltpu.VMEM((peers, tokens, depth), BF16),
            pltpu.VMEM((peers, groups - 1, rows_here, depth), BF16),
            pltpu.VMEM((peers, rows_here, depth), BF16),
            pltpu.VMEM((peers, rows_here, depth), BF16),
            dma,
            dma((chunks,)),
            dma((chunks,)),
            dma((peers,)),
            dma,
            dma,
            dma,
            dma((3, peers, chunks)),
            dma((peers, chunks)),
            dma((peers,)),
            dma((peers,)),
            dma((peers,)),
            dma((peers,)),
            dma((peers,)),
            dma,
            dma,
            dma,
            dma((peers,)),
            dma((peers,)),
            dma((peers,)),
            dma((peers,)),
        ],
        compiler_params=pltpu.CompilerParams(
            collective_id=0, has_side_effects=True, vmem_limit_bytes=56 * 1024 * 1024
        ),
        name="attend_project",
    )(queries, keys, values, log_keep, state_in, norm_gain[None, :], out_weight)
    if layer.ndim == 3:
        layer = layer.transpose(1, 0, 2).reshape(tokens, ratio * depth)
    normed, state, layer = write_out(normed, state, layer)
    return normed, state.reshape(heads, share, width), layer


def write_out(*results):
    pieces = []
    for n, r in enumerate(results):
        cuts = 4 if r.shape[0] % 64 == 0 and r.dtype == BF16 else 1
        rows = r.shape[0] // cuts
        pieces += [(n, i * rows, rows) for i in range(cuts)]

    def body(*refs):
        sems = refs[-1]
        copies = [
            pltpu.make_async_copy(
                refs[n].at[pl.ds(first, rows)],
                refs[len(results) + n].at[pl.ds(first, rows)],
                sems.at[i],
            )
            for i, (n, first, rows) in enumerate(pieces)
        ]
        for copy in copies:
            copy.start()
        for copy in copies:
            copy.wait()

    anywhere = [pl.BlockSpec(memory_space=pl.ANY)] * len(results)
    return pl.pallas_call(
        body,
        out_shape=[jax.ShapeDtypeStruct(r.shape, r.dtype) for r in results],
        in_specs=anywhere,
        out_specs=anywhere,
        scratch_shapes=[pltpu.SemaphoreType.DMA((len(pieces),))],
        name="write_out",
    )(*results)


def solution(mesh):
    peers, groups = mesh.shape["ctx"], mesh.shape["tp"]
    return jax.shard_map(
        functools.partial(per_device, peers, groups),
        mesh=mesh,
        in_specs=(
            P("ctx", "tp"),
            P("ctx", "tp"),
            P("ctx", "tp"),
            P("tp", "ctx"),
            P("tp", None, None),
            P("tp"),
            P("tp", "ctx"),
        ),
        out_specs=(P("ctx", "tp"), P("tp", "ctx", None), P("ctx", "tp")),
        check_vma=False,
    )
```

```python
import functools

import jax
import jax.numpy as jnp
from jax import lax
from jax.experimental import pallas as pl
from jax.experimental.pallas import tpu as pltpu
from jax.sharding import PartitionSpec as P

EPSILON = 1e-06
HIGH = lax.Precision.HIGHEST
MESH = pl.DeviceIdType.MESH
F32 = jnp.float32
BF16 = jnp.bfloat16


def wait_bytes(ref, sem):
    pltpu.make_async_copy(ref, ref, sem).wait()


def dot(a, b, over, precision=None):
    return lax.dot_general(
        a, b, (over, ((), ())), precision=precision, preferred_element_type=F32
    )


def kernel(
    peers, groups, chunks,
    q, k, v, logs, s_in, gain, w_hbm,
    normed, state, layer,
    w, padded, brow, bcol, inc, zst, att, cin, cout, shares, ssq_out, ssq_in,
    acts, parts, arrived, summed, squares, scale, landed, relay,
    w_extra, parts_x, arrived_x, summed_x, relay_x,
    w_sem, chain_s, chain_r, st_s, st_r, sq_s, sq_r, a_s, a_r, rs_s, rs_r, fin_s, mid_r, fwd_s, fin_r,
    wx_s, wx_r, rsx_s, rsx_r, finx_s, midx_r,
):
    c = lax.axis_index("ctx")
    t = lax.axis_index("tp")
    heads, tokens = logs.shape
    width = s_in.shape[1]
    share = state.shape[0] // heads
    chips = peers // 2
    z, j = c // 2, c % 2
    ratio = peers // groups
    rows_here = tokens // groups
    per_chunk = heads // chunks
    last = peers - 1

    split = chips >= 4 and chunks % 2 == 0
    kept = chunks // 2
    half = w.shape[0] // 2
    at_end = jnp.logical_or(z == 0, z == chips - 1)
    beside_end = jnp.logical_or(z == 1, z == chips - 2)
    near_end_chip = jnp.where(z == 1, 0, chips - 1)
    helped = 2 * near_end_chip + j

    def apart(a, b):
        return jnp.logical_or(a - b >= 2, b - a >= 2)

    def far(zk):
        return jnp.logical_and(at_end, apart(zk, z))

    def beyond(zk):
        return jnp.logical_and(beside_end, apart(zk, near_end_chip))

    def goes(g, zk):
        return jnp.logical_not(far(zk)) if split and g >= kept else True

    def goes_up(g, zk):
        limit = chips - 2 if split and g >= kept else chips - 1
        return jnp.logical_and(zk < z, z < limit)

    def goes_down(g, zk):
        limit = 1 if split and g >= kept else 0
        return jnp.logical_and(zk > z, z > limit)

    def remote(src, dst, send, recv, ctx, tp):
        return pltpu.make_async_remote_copy(
            src_ref=src, dst_ref=dst, send_sem=send, recv_sem=recv,
            device_id={"ctx": ctx, "tp": tp}, device_id_type=MESH,
        )

    w_copy = pltpu.make_async_copy(w_hbm, w, w_sem)
    w_copy.start()
    barrier = pltpu.get_barrier_semaphore()
    everyone = peers * groups

    def greet(i, carry):
        other = (c * groups + t + i) % everyone
        pl.semaphore_signal(
            barrier, inc=1,
            device_id={"ctx": other // groups, "tp": other % groups},
            device_id_type=MESH,
        )
        return carry

    lax.fori_loop(1, everyone, greet, 0)

    padded[...] = jnp.zeros_like(padded)
    padded[0:heads, :] = logs[...]
    rows = lax.broadcasted_iota(jnp.int32, (tokens, tokens), 0)
    cols = lax.broadcasted_iota(jnp.int32, (tokens, tokens), 1)
    upper = jnp.where(rows <= cols, 1.0, 0.0).astype(F32)
    by_row = dot(padded[...], upper, ((1,), (0,)), HIGH)
    brow[...] = by_row
    bcol[...] = by_row.T
    lane = lax.broadcasted_iota(jnp.int32, (tokens, 128), 1)

    def column(h):
        return jnp.sum(jnp.where(lane == h, bcol[...], 0.0), axis=1, keepdims=True)

    def head_cols(h):
        return pl.ds(pl.multiple_of(h * width, width), width)

    def head_increment(h, carry):
        hs = head_cols(h)
        summed_logs = column(h)
        factor = jnp.exp(summed_logs[tokens - 1 : tokens] - summed_logs)
        decayed = (k[:, hs].astype(F32) * factor).astype(BF16)
        inc[h] = dot(decayed, v[:, hs], ((0,), (0,)))
        return carry

    lax.fori_loop(0, heads, head_increment, 0, unroll=min(4, heads))
    pl.semaphore_wait(barrier, everyone - 1)

    def hand_over():
        return remote(
            w_hbm.at[pl.ds(half, half)], w_extra, wx_s, wx_r, jnp.where(z == 0, c + 2, c - 2), t
        )

    if split:

        @pl.when(z == chips - 1)
        def _():
            hand_over().start()

    def chain_copy(g):
        part = pl.ds(g * per_chunk, per_chunk)
        return remote(cout.at[part], cin.at[part], chain_s.at[g], chain_r.at[g], c + 1, t)

    def pass_on(g, incoming):
        for h in range(g * per_chunk, (g + 1) * per_chunk):
            start = incoming[h].astype(F32)
            zst[h] = start
            end = jnp.exp(brow[h : h + 1, tokens - 1 : tokens]) * start + inc[h]
            cout[h] = end.astype(BF16)

            @pl.when(c == last)
            def _():
                for to in range(peers):
                    shares[to, h * share : (h + 1) * share, :] = end[to * share : (to + 1) * share]

        @pl.when(c < last)
        def _():
            chain_copy(g).start()

    @pl.when(c == 0)
    def _():
        for g in range(chunks):
            pass_on(g, s_in)

    causal = rows >= cols

    def head_intra(h, carry):
        hs = head_cols(h)
        scores = dot(q[:, hs], k[:, hs], ((1,), (1,)))
        spread = jnp.minimum(column(h) - brow[pl.ds(h, 1), :], 0.0)
        weights = (scores * jnp.where(causal, jnp.exp(spread), 0.0)).astype(BF16)
        att[:, hs] = dot(weights, v[:, hs], ((1,), (0,)))
        return carry

    def intra(g):
        lax.fori_loop(
            g * per_chunk, (g + 1) * per_chunk, head_intra, 0, unroll=min(4, per_chunk)
        )

    sooner = z < chips // 2

    @pl.when(sooner)
    def _():
        intra(0)

    @pl.when(jnp.logical_not(sooner))
    def _():
        lax.fori_loop(0, heads, head_intra, 0, unroll=min(4, heads))

    @pl.when(c > 0)
    def _():
        for g in range(chunks):
            wait_bytes(cin.at[pl.ds(g * per_chunk, per_chunk)], chain_r.at[g])
            pass_on(g, cin)

    def up(s, g):
        return remote(acts.at[s, g], acts.at[s, g], a_s.at[0, s, g], a_r.at[s, g], c + 2, t)

    def down(s, g):
        return remote(acts.at[s, g], acts.at[s, g], a_s.at[1, s, g], a_r.at[s, g], c - 2, t)

    def across(s, g):
        return remote(
            acts.at[s, g], acts.at[s, g], a_s.at[2, s, g], a_r.at[s, g], c + 1 - 2 * j, t
        )

    def state_copy(to):
        return remote(shares.at[to], state, st_s.at[to], st_r, to, t)

    squares[...] = jnp.zeros_like(squares)
    for g in range(chunks):
        if g > 0:

            @pl.when(sooner)
            def _():
                intra(g)

        for i in range(per_chunk):
            h = g * per_chunk + i
            hs = slice(h * width, (h + 1) * width)
            inter = dot(q[:, hs], zst[h].astype(BF16), ((1,), (0,))) * jnp.exp(bcol[:, h : h + 1])
            whole = att[:, hs] + inter
            att[:, hs] = whole
            squares[...] += whole * whole
            acts[c, g, :, i * width : (i + 1) * width] = (whole * gain[:, hs]).astype(BF16)

        @pl.when(z > 0)
        def _():
            down(c, g).start()

        @pl.when(z == 0)
        def _():
            up(c, g).start()

        across(c, g).start()

    @pl.when(jnp.logical_and(z > 0, z < chips - 1))
    def _():
        for g in range(chunks):
            up(c, g).start()

    ssq_out[...] = dot(jnp.ones((8, width), F32), squares[...], ((1,), (1,)), HIGH)
    for off in range(1, groups):
        remote(ssq_out, ssq_in.at[off - 1], sq_s, sq_r, c, (t + off) % groups).start()

    @pl.when(c == last)
    def _():
        for to in range(last):
            state_copy(to).start()
        state[...] = shares[last]

    wait_bytes(ssq_in, sq_r)
    total = ssq_out[...]
    for off in range(1, groups):
        total = total + ssq_in[off - 1]
    spread_total = dot(total, jnp.full((8, width), 0.125, F32), ((0,), (0,)), HIGH)
    scale[...] = lax.rsqrt(spread_total / (groups * heads * width) + EPSILON)

    def head_norm(h, carry):
        hs = head_cols(h)
        normed[:, hs] = (att[:, hs] * scale[...] * gain[:, hs]).astype(BF16)
        return carry

    lax.fori_loop(0, heads, head_norm, 0, unroll=min(4, heads))

    def chip_at(i):
        near_end = jnp.minimum(z, chips - 1 - z)
        half = (i + 1) // 2
        near = jnp.where(i % 2 == 1, z - half, z + half)
        far = jnp.where(z < chips - 1 - z, z + (i - near_end), z - (i - near_end))
        return jnp.where(i <= 2 * near_end, near, far)

    depth = w.shape[1]

    def multiply(s, first, end, weights, rows_used, out):
        rows_of = jnp.concatenate([acts[s, g] for g in range(first, end)], axis=1)
        for n in range(0, depth, 256):
            m = min(n + 256, depth)
            out[s, :, n:m] = dot(rows_of, weights[0:rows_used, n:m], ((1,), (0,))).astype(BF16)

    def scatter(s, out, into, send, recv):
        for off in range(1, groups):
            to = (t + off) % groups
            src = out.at[s, pl.ds(pl.multiple_of(to * rows_here, rows_here), rows_here)]
            remote(src, into.at[s, off - 1], send.at[s], recv.at[s], c, to).start()

    def project(s, zk):
        if split:

            @pl.when(far(zk))
            def _():
                multiply(s, 0, kept, w, half, parts)

            @pl.when(jnp.logical_not(far(zk)))
            def _():
                multiply(s, 0, chunks, w, 2 * half, parts)

        else:
            multiply(s, 0, chunks, w, 2 * half, parts)
        scatter(s, parts, arrived, rs_s, rs_r)

    def project_extra(s):
        multiply(s, kept, chunks, w_extra, half, parts_x)
        scatter(s, parts_x, arrived_x, rsx_s, rsx_r)

    own_rows = pl.ds(pl.multiple_of(t * rows_here, rows_here), rows_here)

    def to_owner(s):
        return remote(summed.at[s], relay.at[c], fin_s.at[s], mid_r.at[c], s, t)

    def gathered_sum(s, out, into, recv):
        wait_bytes(into.at[s], recv.at[s])
        added = out[s, own_rows].astype(F32)
        for off in range(1, groups):
            added = added + into[s, off - 1].astype(F32)
        return added

    def extra_to_owner(s):
        return remote(
            summed_x.at[s], relay_x.at[helped], finx_s.at[s], midx_r.at[helped], s, t
        )

    def finish_extra(s):
        summed_x[s] = gathered_sum(s, parts_x, arrived_x, rsx_r).astype(BF16)
        extra_to_owner(s).start()

    def finish(s):
        added = gathered_sum(s, parts, arrived, rs_r)

        @pl.when(s == c)
        def _():
            relay[c] = added.astype(BF16)

        @pl.when(s != c)
        def _():
            summed[s] = added.astype(BF16)
            to_owner(s).start()

    def to_home(frm):
        return remote(
            relay.at[frm], landed.at[frm % ratio, own_rows], fwd_s.at[frm], fin_r, c, frm // ratio
        )

    def deliver(frm):
        @pl.when(frm != c)
        def _():
            wait_bytes(relay.at[frm], mid_r.at[frm])

        if split:
            source = frm // 2
            from_end = jnp.logical_or(source == 0, source == chips - 1)

            @pl.when(jnp.logical_and(from_end, apart(source, z)))
            def _():
                wait_bytes(relay_x.at[frm], midx_r.at[frm])
                both = relay[frm].astype(F32) + relay_x[frm].astype(F32)
                relay[frm] = both.astype(BF16)

        @pl.when(frm // ratio == t)
        def _():
            pltpu.make_async_copy(relay.at[frm], landed.at[frm % ratio, own_rows], fin_r).start()

        @pl.when(frm // ratio != t)
        def _():
            to_home(frm).start()

    early = chips <= 4

    w_copy.wait()
    first_extra = jnp.where(z == 1, 3, 2)

    if split:

        @pl.when(z == 0)
        def _():
            for g in range(chunks):
                up(c, g).wait_send()
            hand_over().start()

    def step(i, carry):
        zk = chip_at(i)
        s = 2 * zk + j

        @pl.when(i > 0)
        def _():
            for g in range(chunks):

                @pl.when(goes(g, zk))
                def _():
                    wait_bytes(acts.at[s, g], a_r.at[s, g])
                    across(s, g).start()

                @pl.when(goes_up(g, zk))
                def _():
                    up(s, g).start()

                @pl.when(goes_down(g, zk))
                def _():
                    down(s, g).start()

                if g == 0:
                    before = chip_at(i - 1)
                    finish(2 * before + j)
                    finish(2 * before + 1 - j)
                    if early:

                        @pl.when(i > 1)
                        def _():
                            twice = chip_at(i - 2)
                            deliver(2 * twice + j)
                            deliver(2 * twice + 1 - j)

        if split:
            ahead = chip_at(i - 1)

            @pl.when(jnp.logical_and(beside_end, i == first_extra))
            def _():
                wait_bytes(w_extra, wx_r)

            @pl.when(jnp.logical_and(i >= first_extra, beyond(ahead)))
            def _():
                project_extra(2 * ahead + j)
                project_extra(2 * ahead + 1 - j)

        project(s, zk)
        other = 2 * zk + 1 - j
        for g in range(chunks):

            @pl.when(goes(g, zk))
            def _():
                wait_bytes(acts.at[other, g], a_r.at[other, g])

        project(other, zk)
        return carry

    lax.fori_loop(0, chips, step, 0)
    final_chip = chip_at(chips - 1)

    def extra_sums(zk):
        finish_extra(2 * zk + j)
        finish_extra(2 * zk + 1 - j)

    if split:

        @pl.when(beyond(final_chip))
        def _():
            project_extra(2 * final_chip + j)
            project_extra(2 * final_chip + 1 - j)

        def extra_chip(i, carry):
            zk = chip_at(i)

            @pl.when(beyond(zk))
            def _():
                extra_sums(zk)

            return carry

        lax.fori_loop(0, chips - 1, extra_chip, 0)

    finish(2 * final_chip + j)
    finish(2 * final_chip + 1 - j)
    if split:

        @pl.when(beyond(final_chip))
        def _():
            extra_sums(final_chip)

    def deliver_chip(i, carry):
        zk = chip_at(i)
        deliver(2 * zk + j)
        deliver(2 * zk + 1 - j)
        return carry

    lax.fori_loop(max(0, chips - 2) if early else 0, chips, deliver_chip, 0)

    wait_bytes(landed, fin_r)
    for i in range(ratio):
        for n in range(0, depth, 128):
            m = min(n + 128, depth)
            out = (landed[i, :, n:m].astype(F32) * scale[:, 0 : m - n]).astype(BF16)
            if depth % 128 == 0:
                layer[:, i * depth + n : i * depth + m] = out
            else:
                layer[i, :, n:m] = out
    wait_bytes(ssq_in, sq_s)

    @pl.when(c < last)
    def _():
        wait_bytes(state, st_r)
        for g in range(chunks):
            chain_copy(g).wait_send()

    @pl.when(c == last)
    def _():
        for to in range(last):
            state_copy(to).wait_send()

    def drain_chip(zk, carry):
        s = 2 * zk + j

        for g in range(chunks):

            waited = 0 if split else -1

            @pl.when(
                jnp.logical_or(
                    goes_up(g, zk),
                    jnp.logical_and(zk == z, jnp.logical_and(z > waited, z < chips - 1)),
                )
            )
            def _():
                up(s, g).wait_send()

            @pl.when(jnp.logical_or(goes_down(g, zk), jnp.logical_and(zk == z, z > 0)))
            def _():
                down(s, g).wait_send()

            @pl.when(goes(g, zk))
            def _():
                across(s, g).wait_send()

        if split:

            @pl.when(beyond(zk))
            def _():
                for x in (2 * zk, 2 * zk + 1):
                    wait_bytes(arrived_x.at[x], rsx_s.at[x])
                    extra_to_owner(x).wait_send()

        return carry

    if split:

        @pl.when(at_end)
        def _():
            hand_over().wait_send()

    lax.fori_loop(0, chips, drain_chip, 0)

    def drain_slot(s, carry):
        wait_bytes(arrived.at[s], rs_s.at[s])

        @pl.when(s != c)
        def _():
            to_owner(s).wait_send()

        @pl.when(s // ratio != t)
        def _():
            to_home(s).wait_send()

        return carry

    lax.fori_loop(0, peers, drain_slot, 0)


def per_device(peers, groups, queries, keys, values, log_keep, state_in, norm_gain, out_weight):
    heads, tokens = log_keep.shape
    width = state_in.shape[1]
    columns = queries.shape[1]
    depth = out_weight.shape[1]
    chunks = min(4, heads)
    share = width // peers
    ratio = peers // groups
    rows_here = tokens // groups
    dma = pltpu.SemaphoreType.DMA
    vmem = pl.BlockSpec(memory_space=pltpu.VMEM)
    normed, state, layer = pl.pallas_call(
        functools.partial(kernel, peers, groups, chunks),
        out_shape=(
            jax.ShapeDtypeStruct((tokens, columns), BF16),
            jax.ShapeDtypeStruct((heads * share, width), F32),
            jax.ShapeDtypeStruct(
                (tokens, ratio * depth) if depth % 128 == 0 else (ratio, tokens, depth), BF16
            ),
        ),
        in_specs=[vmem] * 6 + [pl.BlockSpec(memory_space=pl.ANY)],
        out_specs=(vmem, vmem, vmem),
        scratch_shapes=[
            pltpu.VMEM(out_weight.shape, BF16),
            pltpu.VMEM((128, tokens), F32),
            pltpu.VMEM((128, tokens), F32),
            pltpu.VMEM((tokens, 128), F32),
            pltpu.VMEM((heads, width, width), F32),
            pltpu.VMEM((heads, width, width), F32),
            pltpu.VMEM((tokens, columns), F32),
            pltpu.VMEM((heads, width, width), BF16),
            pltpu.VMEM((heads, width, width), BF16),
            pltpu.VMEM((peers, heads * share, width), F32),
            pltpu.VMEM((8, tokens), F32),
            pltpu.VMEM((groups - 1, 8, tokens), F32),
            pltpu.VMEM((peers, chunks, tokens, columns // chunks), BF16),
            pltpu.VMEM((peers, tokens, depth), BF16),
            pltpu.VMEM((peers, groups - 1, rows_here, depth), BF16),
            pltpu.VMEM((peers, rows_here, depth), BF16),
            pltpu.VMEM((tokens, width), F32),
            pltpu.VMEM((tokens, width), F32),
            pltpu.VMEM((ratio, tokens, depth), BF16),
            pltpu.VMEM((peers, rows_here, depth), BF16),
            pltpu.VMEM((columns // 2, depth), BF16),
            pltpu.VMEM((peers, tokens, depth), BF16),
            pltpu.VMEM((peers, groups - 1, rows_here, depth), BF16),
            pltpu.VMEM((peers, rows_here, depth), BF16),
            pltpu.VMEM((peers, rows_here, depth), BF16),
            dma,
            dma((chunks,)),
            dma((chunks,)),
            dma((peers,)),
            dma,
            dma,
            dma,
            dma((3, peers, chunks)),
            dma((peers, chunks)),
            dma((peers,)),
            dma((peers,)),
            dma((peers,)),
            dma((peers,)),
            dma((peers,)),
            dma,
            dma,
            dma,
            dma((peers,)),
            dma((peers,)),
            dma((peers,)),
            dma((peers,)),
        ],
        compiler_params=pltpu.CompilerParams(
            collective_id=0, has_side_effects=True, vmem_limit_bytes=56 * 1024 * 1024
        ),
        name="attend_project",
    )(queries, keys, values, log_keep, state_in, norm_gain[None, :], out_weight)
    if layer.ndim == 3:
        layer = layer.transpose(1, 0, 2).reshape(tokens, ratio * depth)
    normed, state, layer = write_out(normed, state, layer)
    return normed, state.reshape(heads, share, width), layer


def write_out(*results):
    pieces = []
    for n, r in enumerate(results):
        cuts = 4 if r.shape[0] % 64 == 0 and r.dtype == BF16 else 1
        rows = r.shape[0] // cuts
        pieces += [(n, i * rows, rows) for i in range(cuts)]

    def body(*refs):
        held, sems = refs[2 * len(results) : -1], refs[-1]

        def part(n, i):
            first, rows = pieces[i][1:]
            return refs[n].at[pl.ds(first, rows)]

        def inward(i):
            n, first, rows = pieces[i]
            return pltpu.make_async_copy(part(n, i), held[n].at[pl.ds(first, rows)], sems.at[0, i])

        def outward(i):
            n, first, rows = pieces[i]
            return pltpu.make_async_copy(
                held[n].at[pl.ds(first, rows)], part(len(results) + n, i), sems.at[1, i]
            )

        for i in range(len(pieces)):
            inward(i).start()
        for i in range(len(pieces)):
            inward(i).wait()
            outward(i).start()
        for i in range(len(pieces)):
            outward(i).wait()

    anywhere = [pl.BlockSpec(memory_space=pl.ANY)] * len(results)
    return pl.pallas_call(
        body,
        out_shape=[jax.ShapeDtypeStruct(r.shape, r.dtype) for r in results],
        in_specs=anywhere,
        out_specs=anywhere,
        scratch_shapes=[pltpu.VMEM(r.shape, r.dtype) for r in results]
        + [pltpu.SemaphoreType.DMA((2, len(pieces)))],
        compiler_params=pltpu.CompilerParams(vmem_limit_bytes=56 * 1024 * 1024),
        name="write_out",
    )(*results)


def solution(mesh):
    peers, groups = mesh.shape["ctx"], mesh.shape["tp"]
    return jax.shard_map(
        functools.partial(per_device, peers, groups),
        mesh=mesh,
        in_specs=(
            P("ctx", "tp"),
            P("ctx", "tp"),
            P("ctx", "tp"),
            P("tp", "ctx"),
            P("tp", None, None),
            P("tp"),
            P("tp", "ctx"),
        ),
        out_specs=(P("ctx", "tp"), P("tp", "ctx", None), P("ctx", "tp")),
        check_vma=False,
    )
```

```python
import functools

import jax
import jax.numpy as jnp
from jax import lax
from jax.experimental import pallas as pl
from jax.experimental.pallas import tpu as pltpu
from jax.sharding import PartitionSpec as P

EPSILON = 1e-06
HIGH = lax.Precision.HIGHEST
MESH = pl.DeviceIdType.MESH
F32 = jnp.float32
BF16 = jnp.bfloat16


def wait_bytes(ref, sem):
    pltpu.make_async_copy(ref, ref, sem).wait()


def dot(a, b, over, precision=None):
    return lax.dot_general(
        a, b, (over, ((), ())), precision=precision, preferred_element_type=F32
    )


def kernel(
    peers, groups, chunks,
    q, k, v, logs, s_in, gain, w_hbm,
    normed, state, layer,
    w, padded, brow, bcol, inc, zst, att, cin, cout, shares, ssq_out, ssq_in,
    acts, parts, arrived, summed, squares, scale, landed, relay,
    w_extra, parts_x, arrived_x, summed_x, relay_x,
    w_sem, chain_s, chain_r, st_s, st_r, sq_s, sq_r, a_s, a_r, rs_s, rs_r, fin_s, mid_r, fwd_s, fin_r,
    wx_s, wx_r, rsx_s, rsx_r, finx_s, midx_r,
):
    c = lax.axis_index("ctx")
    t = lax.axis_index("tp")
    heads, tokens = logs.shape
    width = s_in.shape[1]
    share = state.shape[0] // heads
    chips = peers // 2
    z, j = c // 2, c % 2
    ratio = peers // groups
    rows_here = tokens // groups
    per_chunk = heads // chunks
    last = peers - 1

    split = chips >= 4 and chunks % 2 == 0
    kept = chunks // 2
    half = w.shape[0] // 2
    at_end = jnp.logical_or(z == 0, z == chips - 1)
    beside_end = jnp.logical_or(z == 1, z == chips - 2)
    near_end_chip = jnp.where(z == 1, 0, chips - 1)
    helped = 2 * near_end_chip + j

    def apart(a, b):
        return jnp.logical_or(a - b >= 2, b - a >= 2)

    def far(zk):
        return jnp.logical_and(at_end, apart(zk, z))

    def beyond(zk):
        return jnp.logical_and(beside_end, apart(zk, near_end_chip))

    def goes(g, zk):
        return jnp.logical_not(far(zk)) if split and g >= kept else True

    def goes_up(g, zk):
        limit = chips - 2 if split and g >= kept else chips - 1
        return jnp.logical_and(zk < z, z < limit)

    def goes_down(g, zk):
        limit = 1 if split and g >= kept else 0
        return jnp.logical_and(zk > z, z > limit)

    def remote(src, dst, send, recv, ctx, tp):
        return pltpu.make_async_remote_copy(
            src_ref=src, dst_ref=dst, send_sem=send, recv_sem=recv,
            device_id={"ctx": ctx, "tp": tp}, device_id_type=MESH,
        )

    w_copy = pltpu.make_async_copy(w_hbm, w, w_sem)
    w_copy.start()
    barrier = pltpu.get_barrier_semaphore()
    everyone = peers * groups

    def greet(i, carry):
        other = (c * groups + t + i) % everyone
        pl.semaphore_signal(
            barrier, inc=1,
            device_id={"ctx": other // groups, "tp": other % groups},
            device_id_type=MESH,
        )
        return carry

    lax.fori_loop(1, everyone, greet, 0)

    padded[...] = jnp.zeros_like(padded)
    padded[0:heads, :] = logs[...]
    rows = lax.broadcasted_iota(jnp.int32, (tokens, tokens), 0)
    cols = lax.broadcasted_iota(jnp.int32, (tokens, tokens), 1)
    upper = jnp.where(rows <= cols, 1.0, 0.0).astype(F32)
    by_row = dot(padded[...], upper, ((1,), (0,)), HIGH)
    brow[...] = by_row
    bcol[...] = by_row.T
    lane = lax.broadcasted_iota(jnp.int32, (tokens, 128), 1)

    def column(h):
        return jnp.sum(jnp.where(lane == h, bcol[...], 0.0), axis=1, keepdims=True)

    def head_cols(h):
        return pl.ds(pl.multiple_of(h * width, width), width)

    def head_increment(h, carry):
        hs = head_cols(h)
        summed_logs = column(h)
        factor = jnp.exp(summed_logs[tokens - 1 : tokens] - summed_logs)
        decayed = (k[:, hs].astype(F32) * factor).astype(BF16)
        inc[h] = dot(decayed, v[:, hs], ((0,), (0,)))
        return carry

    lax.fori_loop(0, heads, head_increment, 0, unroll=min(4, heads))
    pl.semaphore_wait(barrier, everyone - 1)

    def hand_over():
        return remote(
            w_hbm.at[pl.ds(half, half)], w_extra, wx_s, wx_r, jnp.where(z == 0, c + 2, c - 2), t
        )

    if split:

        @pl.when(at_end)
        def _():
            hand_over().start()

    def chain_copy(g):
        part = pl.ds(g * per_chunk, per_chunk)
        return remote(cout.at[part], cin.at[part], chain_s.at[g], chain_r.at[g], c + 1, t)

    def pass_on(g, incoming):
        for h in range(g * per_chunk, (g + 1) * per_chunk):
            start = incoming[h].astype(F32)
            zst[h] = start
            end = jnp.exp(brow[h : h + 1, tokens - 1 : tokens]) * start + inc[h]
            cout[h] = end.astype(BF16)

            @pl.when(c == last)
            def _():
                for to in range(peers):
                    shares[to, h * share : (h + 1) * share, :] = end[to * share : (to + 1) * share]

        @pl.when(c < last)
        def _():
            chain_copy(g).start()

    @pl.when(c == 0)
    def _():
        for g in range(chunks):
            pass_on(g, s_in)

    causal = rows >= cols

    def head_intra(h, carry):
        hs = head_cols(h)
        scores = dot(q[:, hs], k[:, hs], ((1,), (1,)))
        spread = jnp.minimum(column(h) - brow[pl.ds(h, 1), :], 0.0)
        weights = (scores * jnp.where(causal, jnp.exp(spread), 0.0)).astype(BF16)
        att[:, hs] = dot(weights, v[:, hs], ((1,), (0,)))
        return carry

    def intra(g):
        lax.fori_loop(
            g * per_chunk, (g + 1) * per_chunk, head_intra, 0, unroll=min(4, per_chunk)
        )

    sooner = z < chips // 2

    @pl.when(sooner)
    def _():
        intra(0)

    @pl.when(jnp.logical_not(sooner))
    def _():
        lax.fori_loop(0, heads, head_intra, 0, unroll=min(4, heads))

    @pl.when(c > 0)
    def _():
        for g in range(chunks):
            wait_bytes(cin.at[pl.ds(g * per_chunk, per_chunk)], chain_r.at[g])
            pass_on(g, cin)

    def up(s, g):
        return remote(acts.at[s, g], acts.at[s, g], a_s.at[0, s, g], a_r.at[s, g], c + 2, t)

    def down(s, g):
        return remote(acts.at[s, g], acts.at[s, g], a_s.at[1, s, g], a_r.at[s, g], c - 2, t)

    def across(s, g):
        return remote(
            acts.at[s, g], acts.at[s, g], a_s.at[2, s, g], a_r.at[s, g], c + 1 - 2 * j, t
        )

    def state_copy(to):
        return remote(shares.at[to], state, st_s.at[to], st_r, to, t)

    squares[...] = jnp.zeros_like(squares)
    for g in range(chunks):
        if g > 0:

            @pl.when(sooner)
            def _():
                intra(g)

        for i in range(per_chunk):
            h = g * per_chunk + i
            hs = slice(h * width, (h + 1) * width)
            inter = dot(q[:, hs], zst[h].astype(BF16), ((1,), (0,))) * jnp.exp(bcol[:, h : h + 1])
            whole = att[:, hs] + inter
            att[:, hs] = whole
            squares[...] += whole * whole
            acts[c, g, :, i * width : (i + 1) * width] = (whole * gain[:, hs]).astype(BF16)

        @pl.when(z > 0)
        def _():
            down(c, g).start()

        @pl.when(z == 0)
        def _():
            up(c, g).start()

        across(c, g).start()

    @pl.when(jnp.logical_and(z > 0, z < chips - 1))
    def _():
        for g in range(chunks):
            up(c, g).start()

    ssq_out[...] = dot(jnp.ones((8, width), F32), squares[...], ((1,), (1,)), HIGH)
    for off in range(1, groups):
        remote(ssq_out, ssq_in.at[off - 1], sq_s, sq_r, c, (t + off) % groups).start()

    @pl.when(c == last)
    def _():
        for to in range(last):
            state_copy(to).start()
        state[...] = shares[last]

    wait_bytes(ssq_in, sq_r)
    total = ssq_out[...]
    for off in range(1, groups):
        total = total + ssq_in[off - 1]
    spread_total = dot(total, jnp.full((8, width), 0.125, F32), ((0,), (0,)), HIGH)
    scale[...] = lax.rsqrt(spread_total / (groups * heads * width) + EPSILON)

    def head_norm(h, carry):
        hs = head_cols(h)
        normed[:, hs] = (att[:, hs] * scale[...] * gain[:, hs]).astype(BF16)
        return carry

    lax.fori_loop(0, heads, head_norm, 0, unroll=min(4, heads))

    def chip_at(i):
        near_end = jnp.minimum(z, chips - 1 - z)
        half = (i + 1) // 2
        near = jnp.where(i % 2 == 1, z - half, z + half)
        far = jnp.where(z < chips - 1 - z, z + (i - near_end), z - (i - near_end))
        return jnp.where(i <= 2 * near_end, near, far)

    depth = w.shape[1]

    def multiply(s, first, end, weights, rows_used, out):
        rows_of = jnp.concatenate([acts[s, g] for g in range(first, end)], axis=1)
        for n in range(0, depth, 256):
            m = min(n + 256, depth)
            out[s, :, n:m] = dot(rows_of, weights[0:rows_used, n:m], ((1,), (0,))).astype(BF16)

    def scatter(s, out, into, send, recv):
        for off in range(1, groups):
            to = (t + off) % groups
            src = out.at[s, pl.ds(pl.multiple_of(to * rows_here, rows_here), rows_here)]
            remote(src, into.at[s, off - 1], send.at[s], recv.at[s], c, to).start()

    def project(s, zk):
        if split:

            @pl.when(far(zk))
            def _():
                multiply(s, 0, kept, w, half, parts)

            @pl.when(jnp.logical_not(far(zk)))
            def _():
                multiply(s, 0, chunks, w, 2 * half, parts)

        else:
            multiply(s, 0, chunks, w, 2 * half, parts)
        scatter(s, parts, arrived, rs_s, rs_r)

    def project_extra(s):
        multiply(s, kept, chunks, w_extra, half, parts_x)
        scatter(s, parts_x, arrived_x, rsx_s, rsx_r)

    own_rows = pl.ds(pl.multiple_of(t * rows_here, rows_here), rows_here)

    def to_owner(s):
        return remote(summed.at[s], relay.at[c], fin_s.at[s], mid_r.at[c], s, t)

    def gathered_sum(s, out, into, recv):
        wait_bytes(into.at[s], recv.at[s])
        added = out[s, own_rows].astype(F32)
        for off in range(1, groups):
            added = added + into[s, off - 1].astype(F32)
        return added

    def extra_to_owner(s):
        return remote(
            summed_x.at[s], relay_x.at[helped], finx_s.at[s], midx_r.at[helped], s, t
        )

    def finish_extra(s):
        summed_x[s] = gathered_sum(s, parts_x, arrived_x, rsx_r).astype(BF16)
        extra_to_owner(s).start()

    def finish(s):
        added = gathered_sum(s, parts, arrived, rs_r)

        @pl.when(s == c)
        def _():
            relay[c] = added.astype(BF16)

        @pl.when(s != c)
        def _():
            summed[s] = added.astype(BF16)
            to_owner(s).start()

    def to_home(frm):
        return remote(
            relay.at[frm], landed.at[frm % ratio, own_rows], fwd_s.at[frm], fin_r, c, frm // ratio
        )

    def deliver(frm):
        @pl.when(frm != c)
        def _():
            wait_bytes(relay.at[frm], mid_r.at[frm])

        if split:
            source = frm // 2
            from_end = jnp.logical_or(source == 0, source == chips - 1)

            @pl.when(jnp.logical_and(from_end, apart(source, z)))
            def _():
                wait_bytes(relay_x.at[frm], midx_r.at[frm])
                both = relay[frm].astype(F32) + relay_x[frm].astype(F32)
                relay[frm] = both.astype(BF16)

        @pl.when(frm // ratio == t)
        def _():
            pltpu.make_async_copy(relay.at[frm], landed.at[frm % ratio, own_rows], fin_r).start()

        @pl.when(frm // ratio != t)
        def _():
            to_home(frm).start()

    early = chips <= 4

    w_copy.wait()
    first_extra = jnp.where(z == 1, 3, 2)

    def step(i, carry):
        zk = chip_at(i)
        s = 2 * zk + j

        @pl.when(i > 0)
        def _():
            for g in range(chunks):

                @pl.when(goes(g, zk))
                def _():
                    wait_bytes(acts.at[s, g], a_r.at[s, g])
                    across(s, g).start()

                @pl.when(goes_up(g, zk))
                def _():
                    up(s, g).start()

                @pl.when(goes_down(g, zk))
                def _():
                    down(s, g).start()

                if g == 0:
                    before = chip_at(i - 1)
                    finish(2 * before + j)
                    finish(2 * before + 1 - j)
                    if early:

                        @pl.when(i > 1)
                        def _():
                            twice = chip_at(i - 2)
                            deliver(2 * twice + j)
                            deliver(2 * twice + 1 - j)

        if split:
            ahead = chip_at(i - 1)

            @pl.when(jnp.logical_and(beside_end, i == first_extra))
            def _():
                wait_bytes(w_extra, wx_r)

            @pl.when(jnp.logical_and(i >= first_extra, beyond(ahead)))
            def _():
                project_extra(2 * ahead + j)
                project_extra(2 * ahead + 1 - j)

        project(s, zk)
        other = 2 * zk + 1 - j
        for g in range(chunks):

            @pl.when(goes(g, zk))
            def _():
                wait_bytes(acts.at[other, g], a_r.at[other, g])

        project(other, zk)
        return carry

    lax.fori_loop(0, chips, step, 0)
    final_chip = chip_at(chips - 1)

    def extra_sums(zk):
        finish_extra(2 * zk + j)
        finish_extra(2 * zk + 1 - j)

    if split:

        @pl.when(beyond(final_chip))
        def _():
            project_extra(2 * final_chip + j)
            project_extra(2 * final_chip + 1 - j)

        def extra_chip(i, carry):
            zk = chip_at(i)

            @pl.when(beyond(zk))
            def _():
                extra_sums(zk)

            return carry

        lax.fori_loop(0, chips - 1, extra_chip, 0)

    finish(2 * final_chip + j)
    finish(2 * final_chip + 1 - j)
    if split:

        @pl.when(beyond(final_chip))
        def _():
            extra_sums(final_chip)

    def deliver_chip(i, carry):
        zk = chip_at(i)
        deliver(2 * zk + j)
        deliver(2 * zk + 1 - j)
        return carry

    lax.fori_loop(max(0, chips - 2) if early else 0, chips, deliver_chip, 0)

    wait_bytes(landed, fin_r)
    for i in range(ratio):
        for n in range(0, depth, 128):
            m = min(n + 128, depth)
            out = (landed[i, :, n:m].astype(F32) * scale[:, 0 : m - n]).astype(BF16)
            if depth % 128 == 0:
                layer[:, i * depth + n : i * depth + m] = out
            else:
                layer[i, :, n:m] = out
    wait_bytes(ssq_in, sq_s)

    @pl.when(c < last)
    def _():
        wait_bytes(state, st_r)
        for g in range(chunks):
            chain_copy(g).wait_send()

    @pl.when(c == last)
    def _():
        for to in range(last):
            state_copy(to).wait_send()

    def drain_chip(zk, carry):
        s = 2 * zk + j

        for g in range(chunks):

            @pl.when(
                jnp.logical_or(
                    goes_up(g, zk),
                    jnp.logical_and(zk == z, z < chips - 1),
                )
            )
            def _():
                up(s, g).wait_send()

            @pl.when(jnp.logical_or(goes_down(g, zk), jnp.logical_and(zk == z, z > 0)))
            def _():
                down(s, g).wait_send()

            @pl.when(goes(g, zk))
            def _():
                across(s, g).wait_send()

        if split:

            @pl.when(beyond(zk))
            def _():
                for x in (2 * zk, 2 * zk + 1):
                    wait_bytes(arrived_x.at[x], rsx_s.at[x])
                    extra_to_owner(x).wait_send()

        return carry

    if split:

        @pl.when(at_end)
        def _():
            hand_over().wait_send()

    lax.fori_loop(0, chips, drain_chip, 0)

    def drain_slot(s, carry):
        wait_bytes(arrived.at[s], rs_s.at[s])

        @pl.when(s != c)
        def _():
            to_owner(s).wait_send()

        @pl.when(s // ratio != t)
        def _():
            to_home(s).wait_send()

        return carry

    lax.fori_loop(0, peers, drain_slot, 0)


def per_device(peers, groups, queries, keys, values, log_keep, state_in, norm_gain, out_weight):
    heads, tokens = log_keep.shape
    width = state_in.shape[1]
    columns = queries.shape[1]
    depth = out_weight.shape[1]
    chunks = min(4, heads)
    share = width // peers
    ratio = peers // groups
    rows_here = tokens // groups
    dma = pltpu.SemaphoreType.DMA
    vmem = pl.BlockSpec(memory_space=pltpu.VMEM)
    normed, state, layer = pl.pallas_call(
        functools.partial(kernel, peers, groups, chunks),
        out_shape=(
            jax.ShapeDtypeStruct((tokens, columns), BF16),
            jax.ShapeDtypeStruct((heads * share, width), F32),
            jax.ShapeDtypeStruct(
                (tokens, ratio * depth) if depth % 128 == 0 else (ratio, tokens, depth), BF16
            ),
        ),
        in_specs=[vmem] * 6 + [pl.BlockSpec(memory_space=pl.ANY)],
        out_specs=(vmem, vmem, vmem),
        scratch_shapes=[
            pltpu.VMEM(out_weight.shape, BF16),
            pltpu.VMEM((128, tokens), F32),
            pltpu.VMEM((128, tokens), F32),
            pltpu.VMEM((tokens, 128), F32),
            pltpu.VMEM((heads, width, width), F32),
            pltpu.VMEM((heads, width, width), F32),
            pltpu.VMEM((tokens, columns), F32),
            pltpu.VMEM((heads, width, width), BF16),
            pltpu.VMEM((heads, width, width), BF16),
            pltpu.VMEM((peers, heads * share, width), F32),
            pltpu.VMEM((8, tokens), F32),
            pltpu.VMEM((groups - 1, 8, tokens), F32),
            pltpu.VMEM((peers, chunks, tokens, columns // chunks), BF16),
            pltpu.VMEM((peers, tokens, depth), BF16),
            pltpu.VMEM((peers, groups - 1, rows_here, depth), BF16),
            pltpu.VMEM((peers, rows_here, depth), BF16),
            pltpu.VMEM((tokens, width), F32),
            pltpu.VMEM((tokens, width), F32),
            pltpu.VMEM((ratio, tokens, depth), BF16),
            pltpu.VMEM((peers, rows_here, depth), BF16),
            pltpu.VMEM((columns // 2, depth), BF16),
            pltpu.VMEM((peers, tokens, depth), BF16),
            pltpu.VMEM((peers, groups - 1, rows_here, depth), BF16),
            pltpu.VMEM((peers, rows_here, depth), BF16),
            pltpu.VMEM((peers, rows_here, depth), BF16),
            dma,
            dma((chunks,)),
            dma((chunks,)),
            dma((peers,)),
            dma,
            dma,
            dma,
            dma((3, peers, chunks)),
            dma((peers, chunks)),
            dma((peers,)),
            dma((peers,)),
            dma((peers,)),
            dma((peers,)),
            dma((peers,)),
            dma,
            dma,
            dma,
            dma((peers,)),
            dma((peers,)),
            dma((peers,)),
            dma((peers,)),
        ],
        compiler_params=pltpu.CompilerParams(
            collective_id=0, has_side_effects=True, vmem_limit_bytes=56 * 1024 * 1024
        ),
        name="attend_project",
    )(queries, keys, values, log_keep, state_in, norm_gain[None, :], out_weight)
    if layer.ndim == 3:
        layer = layer.transpose(1, 0, 2).reshape(tokens, ratio * depth)
    normed, state, layer = write_out(normed, state, layer)
    return normed, state.reshape(heads, share, width), layer


def write_out(*results):
    pieces = []
    for n, r in enumerate(results):
        cuts = 4 if r.shape[0] % 64 == 0 and r.dtype == BF16 else 1
        rows = r.shape[0] // cuts
        pieces += [(n, i * rows, rows) for i in range(cuts)]

    def body(*refs):
        held, sems = refs[2 * len(results) : -1], refs[-1]

        def part(n, i):
            first, rows = pieces[i][1:]
            return refs[n].at[pl.ds(first, rows)]

        def inward(i):
            n, first, rows = pieces[i]
            return pltpu.make_async_copy(part(n, i), held[n].at[pl.ds(first, rows)], sems.at[0, i])

        def outward(i):
            n, first, rows = pieces[i]
            return pltpu.make_async_copy(
                held[n].at[pl.ds(first, rows)], part(len(results) + n, i), sems.at[1, i]
            )

        for i in range(len(pieces)):
            inward(i).start()
        for i in range(len(pieces)):
            inward(i).wait()
            outward(i).start()
        for i in range(len(pieces)):
            outward(i).wait()

    anywhere = [pl.BlockSpec(memory_space=pl.ANY)] * len(results)
    return pl.pallas_call(
        body,
        out_shape=[jax.ShapeDtypeStruct(r.shape, r.dtype) for r in results],
        in_specs=anywhere,
        out_specs=anywhere,
        scratch_shapes=[pltpu.VMEM(r.shape, r.dtype) for r in results]
        + [pltpu.SemaphoreType.DMA((2, len(pieces)))],
        compiler_params=pltpu.CompilerParams(vmem_limit_bytes=56 * 1024 * 1024),
        name="write_out",
    )(*results)


def solution(mesh):
    peers, groups = mesh.shape["ctx"], mesh.shape["tp"]
    return jax.shard_map(
        functools.partial(per_device, peers, groups),
        mesh=mesh,
        in_specs=(
            P("ctx", "tp"),
            P("ctx", "tp"),
            P("ctx", "tp"),
            P("tp", "ctx"),
            P("tp", None, None),
            P("tp"),
            P("tp", "ctx"),
        ),
        out_specs=(P("ctx", "tp"), P("tp", "ctx", None), P("ctx", "tp")),
        check_vma=False,
    )
```
